128 devices in a mesh: ctx: 64 (over y_lo, z, x, core), batch: 2 (over y_hi).
Axes of the slice: x: 4, y: 4 (y_hi: 2, y_lo: 2; y = y_hi * 2 + y_lo), z: 4, core: 2. Of those that a mesh axis runs over, the one named last changes fastest.
Arguments:
- context: bfloat16 [32768, 2048], P(('batch', 'ctx')), parts along dimension 0, may hold values from -48 to 48
- norm_gain: float32 [2048], replicated, may hold values from 0.1 to 1.9
- query_weight: bfloat16 [2048, 1024], replicated, may hold values from -1 to 1
- key_weight: bfloat16 [2048, 1024], replicated, may hold values from -1 to 1
- value_weight: bfloat16 [2048, 1024], replicated, may hold values from -0.125 to 0.125
- out_weight: bfloat16 [1024, 2048], replicated, may hold values from -3 to 3
Outputs:
- output: bfloat16 [512, 2048], P(('batch', 'ctx')), parts along dimension 0
The draws below stay inside these ranges and needn't reach their ends.
There are 2 independent parts, one for each index of `batch`. The reference program is written for one: setup_inputs(seed, part) draws one part's arguments, and reference() takes and returns one part's arrays. A program takes and returns all parts, laid end to end along the dimension named above; an argument that names none is the same for every part. Nothing has to cross between parts.
All inputs are finite; a program needn't handle non-finite values.
Results may differ from the reference program's by a relative error of at most 0.013.
Values may be sent and summed in bfloat16 or wider, within the bound.
No kernel may reach another device: no remote copies, remote signals or barrier semaphores. Data moves between devices by JAX's collectives and lax.ppermute only.
A program may use at most 320 MiB of HBM per device.

```python
import math
import jax
import jax.numpy as jnp
from jax import lax

D = 2048
HEADS = 8
HD = 128
HQ = 1024
LAT = 256
CTX = 16384


def draw_query_weight(key, part):
    key = jax.random.fold_in(key, 1)
    noise = jnp.clip(jax.random.normal(key, (D, HQ), jnp.float32), -5.0, 5.0)
    mixed = noise
    return jnp.clip(mixed * math.sqrt(2.0 / D), -1.0, 1.0).astype(jnp.bfloat16)


def draw_key_weight(key, part):
    key = jax.random.fold_in(key, 2)
    noise = jnp.clip(jax.random.normal(key, (D, HQ), jnp.float32), -5.0, 5.0)
    mixed = noise
    return jnp.clip(mixed * math.sqrt(2.0 / D), -1.0, 1.0).astype(jnp.bfloat16)


def draw_context(key, part):
    key = jax.random.fold_in(key, 3)
    streams = jax.random.split(key, 3)
    column_scale = jnp.exp(jax.random.uniform(streams[0], (1, D), jnp.float32, 0.0, math.log(10.0)))
    entries = jnp.clip(jax.random.normal(streams[1], (CTX, D), jnp.float32), -4.8, 4.8)
    row_scale = jnp.exp(jax.random.uniform(streams[2], (CTX, 1), jnp.float32, 0.0, math.log(10.0)))
    drawn = row_scale * column_scale * entries * 0.1
    return jnp.clip(drawn, -48.0, 48.0).astype(jnp.bfloat16)


def normal_values(key, dims, width, bound, kind=jnp.bfloat16):
    result = width * jax.random.normal(key, dims, jnp.float32)
    return jnp.clip(result, min=-bound, max=bound).astype(kind)


def setup_inputs(seed: int = 0, part: int = 0) -> dict:
    streams_of = jax.random.split(jax.random.key(seed), 7)
    part_keys = jax.random.split(jax.random.fold_in(streams_of[6], part), 7)
    return {
        "context": draw_context(jax.random.fold_in(jax.random.fold_in(streams_of[6], part), 71), part),
        "norm_gain": jnp.clip(1.0 + 0.18 * jax.random.normal(streams_of[1], (D,), jnp.float32), 0.1, 1.9),
        "query_weight": draw_query_weight(jax.random.fold_in(streams_of[6], 71), part),
        "key_weight": draw_key_weight(jax.random.fold_in(streams_of[6], 71), part),
        "value_weight": normal_values(streams_of[4], (D, HQ), D ** -0.5, 0.125),
        "out_weight": normal_values(streams_of[5], (HQ, D), (max(1, HQ // 256)) ** -0.5, 3.0),
    }


def layer_norm(token_rows, norm_gain):
    widened = token_rows.astype(jnp.float32)
    centred = widened - lax.optimization_barrier(jnp.mean(widened, axis=-1, keepdims=True))
    variance = lax.optimization_barrier(jnp.mean(centred * centred, axis=-1, keepdims=True))
    return (centred * lax.rsqrt(variance + 1e-05) * norm_gain).astype(jnp.bfloat16)

def reference(context, norm_gain, query_weight, key_weight, value_weight, out_weight):
    normed = layer_norm(context, norm_gain)
    latent_rows = normed[CTX - LAT:]
    queries = (jnp.dot(latent_rows, query_weight, preferred_element_type=jnp.float32) * HD ** (-0.5)).astype(jnp.bfloat16)
    keys = jnp.dot(normed, key_weight, preferred_element_type=jnp.float32).astype(jnp.bfloat16)
    values = jnp.dot(normed, value_weight, preferred_element_type=jnp.float32).astype(jnp.bfloat16)
    query_heads = queries.reshape(LAT, HEADS, HD).transpose(1, 0, 2)
    key_heads = keys.reshape(CTX, HEADS, HD).transpose(1, 0, 2)
    value_heads = values.reshape(CTX, HEADS, HD).transpose(1, 0, 2)
    visible = jnp.arange(CTX)[None, :] <= (CTX - LAT + jnp.arange(LAT))[:, None]

    def one_head(operands):
        query_part, key_part, value_part = operands
        scores = jnp.dot(query_part, key_part.T, preferred_element_type=jnp.float32)
        scores = jnp.where(visible, scores, -jnp.inf)
        peak = lax.optimization_barrier(jnp.max(scores, axis=-1, keepdims=True))
        expo = jnp.exp(scores - peak)
        total = lax.optimization_barrier(jnp.sum(expo, axis=-1, keepdims=True))
        weighted = jnp.dot(expo.astype(jnp.bfloat16), value_part, preferred_element_type=jnp.float32)
        return weighted / total
    per_head = lax.map(one_head, (query_heads, key_heads, value_heads))
    attended = per_head.transpose(1, 0, 2).reshape(LAT, HQ).astype(jnp.bfloat16)
    return jnp.dot(attended, out_weight, preferred_element_type=jnp.float32).astype(jnp.bfloat16)
```

```python
import functools

import jax
import jax.numpy as jnp
from jax import lax
from jax.experimental import pallas as pl
from jax.experimental.pallas import tpu as pltpu
from jax.sharding import Mesh
from jax.sharding import PartitionSpec as P

HEADS = 8
HD = 128
D = 2048
LAT = 256
ROWS = 256
CTX = 16384
MINE = 4
F32 = jnp.float32
BF16 = jnp.bfloat16
CTX_AXES = ("yl", "z", "x", "core")
SWAP = ((0, 1), (1, 0))
ANY = pl.BlockSpec(memory_space=pl.ANY)
VMEM = pl.BlockSpec(memory_space=pltpu.VMEM)
SMEM = pl.BlockSpec(memory_space=pltpu.SMEM)


def xor_pairs(size, mask):
    return [(i, i ^ mask) for i in range(size)]


def near(i):
    return (i ^ (i >> 1)) & 1


def head_of(yl, z, x, core):
    return core * 4 + (near(x) ^ yl) * 2 + (near(z) ^ yl)


def params(mib):
    return pltpu.CompilerParams(vmem_limit_bytes=mib * 2**20)


def normalise(tokens, gain):
    widened = tokens.astype(F32)
    centred = widened - jnp.mean(widened, axis=-1, keepdims=True)
    variance = jnp.mean(centred * centred, axis=-1, keepdims=True)
    return (centred * lax.rsqrt(variance + 1e-05) * gain).astype(BF16)


def norm_rows(src, gain_ref, dst):
    step = 32

    @pl.loop(0, ROWS // step)
    def _(i):
        at = pl.ds(pl.multiple_of(i * step, step), step)
        dst[at, :] = normalise(src[at, :], gain_ref[...])


def own_kernel(tokens, gain_ref, out):
    norm_rows(tokens, gain_ref, out)


def query_kernel(info, tokens, own, gain_ref, weight, out, q0, q1, q2, q3, wbuf, sems):
    copies = []
    for j in range(4):
        at = pl.ds(pl.multiple_of(info[1 + j] * HD, HD), HD)
        copies.append(pltpu.make_async_copy(weight.at[:, at], wbuf.at[:, pl.ds(j * HD, HD)], sems.at[j]))
        copies[-1].start()
    norm_rows(tokens, gain_ref, out)
    for copy in copies:
        copy.wait()
    scale = HD ** (-0.5)

    def project(rows):
        queries = (jnp.dot(rows[...], wbuf[...], preferred_element_type=F32) * scale).astype(BF16)
        for j, q in enumerate((q0, q1, q2, q3)):
            q[...] = queries[:, j * HD : (j + 1) * HD]

    @pl.when(info[0] == 1)
    def _():
        project(own)

    @pl.when(info[0] == 0)
    def _():
        project(out)


def kv_kernel(info, own, other, wk, wv, o0, o1, o2, o3, wbuf, sems):
    copies = []
    for j in (1, 2, 3, 0):
        at = pl.ds(pl.multiple_of(info[1 + j] * HD, HD), HD)
        pair = []
        for k, weight in enumerate((wk, wv)):
            pair.append(
                pltpu.make_async_copy(weight.at[:, at], wbuf.at[j, :, pl.ds(k * HD, HD)], sems.at[j, k])
            )
            pair[-1].start()
        copies.append(pair)
    for j, out, pair in zip((1, 2, 3, 0), (o1, o2, o3, o0), copies):
        for copy in pair:
            copy.wait()
        for k, rows in enumerate((own, other)):
            out[pl.ds(k * ROWS, ROWS), :] = jnp.dot(
                rows[...], wbuf[j], preferred_element_type=F32
            ).astype(BF16)


def attend_kernel(info, query, kv0, kv1, kv2, kv3, out):
    queries = query[...]
    chunks = (kv0, kv1, kv2, kv3)
    row = lax.broadcasted_iota(jnp.int32, (LAT, ROWS), 0)
    column = lax.broadcasted_iota(jnp.int32, (LAT, ROWS), 1)
    lead = column - row
    scores = []
    for j, kv in enumerate(chunks):
        for half in range(2):
            keys = kv[pl.ds(half * ROWS, ROWS), pl.ds(0, HD)]
            part = lax.dot_general(queries, keys, (((1,), (1,)), ((), ())), preferred_element_type=F32)
            room = CTX - LAT - info[5 + 2 * j + half]
            scores.append(jnp.where(lead <= room, part, -jnp.inf))
    peak = functools.reduce(jnp.maximum, scores)
    peak = jnp.max(peak, axis=-1, keepdims=True)
    total = jnp.zeros((LAT, 1), F32)
    accum = jnp.zeros((LAT, HD), F32)
    for j, kv in enumerate(chunks):
        for half in range(2):
            expo = jnp.exp(scores[2 * j + half] - peak)
            total += jnp.sum(expo, axis=-1, keepdims=True)
            values = kv[pl.ds(half * ROWS, ROWS), pl.ds(HD, HD)]
            accum += jnp.dot(expo.astype(BF16), values, preferred_element_type=F32)
    lane = lax.broadcasted_iota(jnp.int32, (LAT, HD), 1)
    stats = jnp.where(lane < HD // 2, peak, total).reshape(LAT // 8, 8, HD)
    accum = accum.reshape(LAT // 8, 8, HD)
    upper = lax.broadcasted_iota(jnp.int32, (LAT // 8, 8, HD), 1) < MINE
    out[:, 0] = jnp.where(upper, accum, pltpu.roll(stats, MINE, 1))
    out[:, 1] = jnp.where(upper, pltpu.roll(accum, MINE, 1), stats)


def merge_kernel(parts, weight, out):
    lane = lax.broadcasted_iota(jnp.int32, (8, HD), 1) < HD // 2
    row = lax.broadcasted_iota(jnp.int32, (8, HD), 0) < MINE
    members = [[] for _ in range(HEADS)]
    for yl in range(2):
        for z in range(4):
            for x in range(4):
                for core in range(2):
                    members[head_of(yl, z, x, core)].append(((yl * 4 + z) * 4 + x) * 2 + core)
    heads = []
    for group in members:
        accums, peaks, totals = [], [], []
        for source in group:
            block = parts[source]
            stats = pltpu.roll(block, MINE, 0)
            turned = pltpu.roll(stats, HD // 2, 1)
            accums.append(block)
            peaks.append(jnp.where(lane, stats, turned))
            totals.append(jnp.where(lane, turned, stats))
        peak = functools.reduce(jnp.maximum, peaks)
        accum = jnp.zeros((8, HD), F32)
        total = jnp.zeros((8, HD), F32)
        for a, p, t in zip(accums, peaks, totals):
            factor = jnp.exp(p - peak)
            accum += a * factor
            total += t * factor
        heads.append(jnp.where(row, accum / total, 0.0).astype(BF16))
    attended = jnp.concatenate(heads, axis=1)
    result = jnp.dot(attended, weight[...], preferred_element_type=F32).astype(BF16)
    out[...] = result[:MINE]


def shape(*dims, dtype=BF16):
    return jax.ShapeDtypeStruct(dims, dtype)


def local(context, norm_gain, query_weight, key_weight, value_weight, out_weight):
    core = lax.axis_index("core")
    x = lax.axis_index("x")
    z = lax.axis_index("z")
    yl = lax.axis_index("yl")
    gain = norm_gain.reshape(1, D)

    chips = [(yl, z, x), (yl, z, x ^ 1), (yl, z ^ 1, x), (yl ^ 1, z, x)]
    info = [core]
    info += [head_of(b, c, a, core) for b, c, a in chips]
    for b, c, a in chips:
        for half in range(2):
            info.append((((b * 4 + c) * 4 + a) * 2 + (core ^ half)) * ROWS)
    info = jnp.stack(info).astype(jnp.int32)

    other_raw = lax.ppermute(context, "core", SWAP)
    own = pl.pallas_call(
        own_kernel,
        out_shape=shape(ROWS, D),
        in_specs=[VMEM, VMEM],
        out_specs=VMEM,
        compiler_params=params(16),
        cost_estimate=pl.CostEstimate(flops=2**23, bytes_accessed=2**21, transcendentals=0),
    )(context, gain)
    other, *queries = pl.pallas_call(
        query_kernel,
        out_shape=[shape(ROWS, D)] + [shape(LAT, HD)] * 4,
        in_specs=[SMEM, VMEM, VMEM, VMEM, ANY],
        out_specs=[VMEM] * 5,
        scratch_shapes=[pltpu.VMEM((D, 4 * HD), BF16), pltpu.SemaphoreType.DMA((4,))],
        compiler_params=params(24),
        cost_estimate=pl.CostEstimate(flops=2**29, bytes_accessed=2**22, transcendentals=0),
    )(info, other_raw, own, gain, query_weight)

    def hop(value, dx, dz, dy):
        pairs = []
        for b in range(2):
            for c in range(4):
                for a in range(4):
                    pairs.append(((b * 4 + c) * 4 + a, ((b ^ dy) * 4 + (c ^ dz)) * 4 + (a ^ dx)))
        return lax.ppermute(value, ("yl", "z", "x"), pairs)

    dx1, dx3, dz1, dz3, dy = near(x), (x >> 1) ^ 1, near(z), (z >> 1) ^ 1, yl ^ 1
    by_x = hop(queries[1], 1, 0, 0)
    by_z = hop(queries[2], 0, 1, 0)
    by_y = hop(queries[3], 0, 0, 1)

    kv = pl.pallas_call(
        kv_kernel,
        out_shape=[shape(2 * ROWS, 2 * HD)] * 4,
        in_specs=[SMEM, VMEM, VMEM, ANY, ANY],
        out_specs=[VMEM] * 4,
        scratch_shapes=[pltpu.VMEM((4, D, 2 * HD), BF16), pltpu.SemaphoreType.DMA((4, 2))],
        compiler_params=params(24),
        cost_estimate=pl.CostEstimate(flops=2**31, bytes_accessed=2**23, transcendentals=0),
    )(info, own, other, key_weight, value_weight)

    query = jnp.where(dx1 == 1, by_x, jnp.where(dz1 == 1, by_z, jnp.where(dy == 1, by_y, queries[0])))
    far_x, far_z, far_xz = hop(query, 3, 0, 0), hop(query, 0, 3, 0), hop(query, 3, 3, 0)
    kv_x = hop(kv[1], 1, 0, 0)
    kv_z = hop(kv[2], 0, 1, 0)
    kv_y = hop(kv[3], 0, 0, 1)
    query = jnp.where(
        dx3 == 1, jnp.where(dz3 == 1, far_xz, far_x), jnp.where(dz3 == 1, far_z, query)
    )
    across = hop(query, 1, 1, 1)
    query = jnp.where(dx1 + dz1 + dy >= 2, across, query)

    parts = pl.pallas_call(
        attend_kernel,
        out_shape=shape(LAT // 8, 2, 8, HD, dtype=F32),
        in_specs=[SMEM] + [VMEM] * 5,
        out_specs=VMEM,
        compiler_params=params(24),
        cost_estimate=pl.CostEstimate(flops=2**28, bytes_accessed=2**21, transcendentals=2**19),
    )(info, query, kv[0], kv_x, kv_z, kv_y)
    parts = lax.all_to_all(parts.reshape(64, 8, HD), CTX_AXES, 0, 0)
    return pl.pallas_call(
        merge_kernel,
        out_shape=shape(MINE, D),
        in_specs=[VMEM, VMEM],
        out_specs=VMEM,
        compiler_params=params(24),
        cost_estimate=pl.CostEstimate(flops=2**25, bytes_accessed=2**22, transcendentals=2**16),
    )(parts, out_weight)


def solution(mesh):
    fine = Mesh(mesh.devices.reshape(2, 4, 4, 2, 2), CTX_AXES + ("batch",))
    rows = P(("batch",) + CTX_AXES, None)
    return jax.shard_map(
        local,
        mesh=fine,
        in_specs=(rows, P(), P(), P(), P(), P()),
        out_specs=rows,
        check_vma=False,
    )
```

```python
import functools

import jax
import jax.numpy as jnp
from jax import lax
from jax.experimental import pallas as pl
from jax.experimental.pallas import tpu as pltpu
from jax.sharding import Mesh
from jax.sharding import PartitionSpec as P

HEADS = 8
HD = 128
D = 2048
LAT = 256
ROWS = 256
CTX = 16384
MINE = 4
FETCHED = 2
F32 = jnp.float32
BF16 = jnp.bfloat16
CTX_AXES = ("yl", "z", "xh", "xl", "core")
SWAP = ((0, 1), (1, 0))
HBM = pl.BlockSpec(memory_space=pltpu.HBM)
VMEM = pl.BlockSpec(memory_space=pltpu.VMEM)
SMEM = pl.BlockSpec(memory_space=pltpu.SMEM)


def near(i):
    return (i ^ (i >> 1)) & 1


def head_of(yl, z, x, core):
    return core * 4 + near(x) * 2 + yl


def params(mib):
    return pltpu.CompilerParams(vmem_limit_bytes=mib * 2**20)


def normalise(tokens, gain):
    widened = tokens.astype(F32)
    centred = widened - jnp.mean(widened, axis=-1, keepdims=True)
    variance = jnp.mean(centred * centred, axis=-1, keepdims=True)
    return (centred * lax.rsqrt(variance + 1e-05) * gain).astype(BF16)


def fetch_heads(weight, heads, dst, offset, sem):
    at = pl.ds(pl.multiple_of(heads * HD, HD), HD)
    copy = pltpu.make_async_copy(weight.at[:, at], dst.at[:, pl.ds(offset, HD)], sem)
    copy.start()
    return copy


def own_kernel(info, tokens, gain_ref, wq, wk, wv, out, columns, gain, kv_columns, rows, sems):
    first = pltpu.make_async_copy(tokens, rows, sems.at[12])
    first.start()
    second = pltpu.make_async_copy(gain_ref, gain, sems.at[13])
    second.start()
    copies = [fetch_heads(wq, info[1 + j], columns, j * HD, sems.at[j]) for j in range(4)]
    for j in range(4):
        for k, weight in enumerate((wk, wv)):
            copies.append(
                fetch_heads(weight, info[1 + j], kv_columns, (2 * j + k) * HD, sems.at[4 + 2 * j + k])
            )
    first.wait()
    second.wait()
    out[...] = normalise(rows[...], gain[...])
    for copy in copies:
        copy.wait()


def query_kernel(info, tokens, own, gain, weight, out, q0, q1, q2, q3):
    out[...] = normalise(tokens[...], gain[...])
    latents = jnp.where(info[0] == 1, own[...], out[...])
    queries = jnp.dot(latents, weight[...], preferred_element_type=F32) * HD ** (-0.5)
    queries = queries.astype(BF16)
    for j, q in enumerate((q0, q1, q2, q3)):
        q[...] = queries[:, j * HD : (j + 1) * HD]


def kv_kernel(own, other, weight, out, done, sems):
    writes = []
    for k, rows in enumerate((own, other)):
        at = pl.ds(k * ROWS, ROWS)
        projected = jnp.dot(rows[...], weight[...], preferred_element_type=F32).astype(BF16)
        for j in range(4):
            done[j, at, :] = projected[:, j * 2 * HD : (j + 1) * 2 * HD]
        writes.append(pltpu.make_async_copy(done.at[:, at], out.at[:, at], sems.at[k]))
        writes[-1].start()
    for write in writes:
        write.wait()


def fetch_kernel(wo, *rest):
    *pieces, sems = rest
    copies = []
    for j, piece in enumerate(pieces):
        copies.append(pltpu.make_async_copy(wo.at[pl.ds(j * 2 * HD, 2 * HD)], piece, sems.at[j]))
        copies[-1].start()
    for copy in copies:
        copy.wait()


def thirds(value):
    first = value.astype(BF16).astype(F32)
    second = (value - first).astype(BF16).astype(F32)
    return [first, second, value - first - second]


def attend_kernel(info, query, kv, out):
    queries = query[...]
    row = lax.broadcasted_iota(jnp.int32, (LAT, ROWS), 0)
    column = lax.broadcasted_iota(jnp.int32, (LAT, ROWS), 1)
    lead = column - row
    scores = []
    for j in range(4):
        for half in range(2):
            keys = kv[j, pl.ds(half * ROWS, ROWS), pl.ds(0, HD)]
            part = lax.dot_general(queries, keys, (((1,), (1,)), ((), ())), preferred_element_type=F32)
            room = CTX - LAT - info[5 + 2 * j + half]
            scores.append(jnp.where(lead <= room, part, -jnp.inf))
    peak = functools.reduce(jnp.maximum, scores)
    peak = jnp.max(peak, axis=-1, keepdims=True)
    total = jnp.zeros((LAT, 1), F32)
    accum = jnp.zeros((LAT, HD), F32)
    for j in range(4):
        for half in range(2):
            expo = jnp.exp(scores[2 * j + half] - peak)
            total += jnp.sum(expo, axis=-1, keepdims=True)
            values = kv[j, pl.ds(half * ROWS, ROWS), pl.ds(HD, HD)]
            accum += jnp.dot(expo.astype(BF16), values, preferred_element_type=F32)
    lane = lax.broadcasted_iota(jnp.int32, (LAT, HD), 1)
    stats = jnp.zeros((LAT, HD), F32)
    for k, piece in enumerate(thirds(peak) + thirds(total)):
        stats = jnp.where(lane == k, piece, stats)
    stats = stats.reshape(LAT // 8, 8, HD)
    accum = accum.reshape(LAT // 8, 8, HD)
    upper = lax.broadcasted_iota(jnp.int32, (LAT // 8, 8, HD), 1) < MINE
    out[:, 0] = jnp.where(upper, accum, pltpu.roll(stats, MINE, 1)).astype(BF16)
    out[:, 1] = jnp.where(upper, pltpu.roll(accum, MINE, 1), stats).astype(BF16)


def merge_kernel(parts, weight, *rest):
    *pieces, out, wbuf, sems = rest
    copies = []
    for j in range(4 - FETCHED):
        at = pl.ds((FETCHED + j) * 2 * HD, 2 * HD)
        copies.append(pltpu.make_async_copy(weight.at[at], wbuf.at[j], sems.at[j]))
        copies[-1].start()
    row = lax.broadcasted_iota(jnp.int32, (8, HD), 0) < MINE
    k = lax.broadcasted_iota(jnp.int32, (HD, 2 * HD), 0)
    n = lax.broadcasted_iota(jnp.int32, (HD, 2 * HD), 1)
    lead = k - jnp.where(n < HD, 0, 3)
    pick = jnp.where((lead >= 0) & (lead < 3), 1.0, 0.0).astype(BF16)
    stats = jnp.dot(parts[...].reshape(8 * 64, HD), pick, preferred_element_type=F32)
    stats = stats.reshape(64, 8, 2 * HD)
    members = [[] for _ in range(HEADS)]
    for yl in range(2):
        for z in range(4):
            for x in range(4):
                for core in range(2):
                    members[head_of(yl, z, x, core)].append(((yl * 4 + z) * 4 + x) * 2 + core)
    heads = []
    for group in members:
        accums, peaks, totals = [], [], []
        for source in group:
            block = pltpu.roll(stats[source], MINE, 0)
            accums.append(parts[source].astype(F32))
            peaks.append(block[:, :HD])
            totals.append(block[:, HD:])
        peak = functools.reduce(jnp.maximum, peaks)
        accum = jnp.zeros((8, HD), F32)
        total = jnp.zeros((8, HD), F32)
        for a, p, t in zip(accums, peaks, totals):
            factor = jnp.exp(p - peak)
            accum += a * factor
            total += t * factor
        heads.append(jnp.where(row, accum / total, 0.0).astype(BF16))
    result = jnp.zeros((8, D), F32)
    for j in range(4):
        attended = jnp.concatenate(heads[2 * j : 2 * j + 2], axis=1)
        if j < FETCHED:
            rows = pieces[j][...]
        else:
            copies[j - FETCHED].wait()
            rows = wbuf[j - FETCHED]
        result += jnp.dot(attended, rows, preferred_element_type=F32)
    out[...] = result.astype(BF16)[:MINE]


def shape(*dims, dtype=BF16):
    return jax.ShapeDtypeStruct(dims, dtype)


def local(context, norm_gain, query_weight, key_weight, value_weight, out_weight):
    core = lax.axis_index("core")
    x = lax.axis_index(("xh", "xl"))
    z = lax.axis_index("z")
    yl = lax.axis_index("yl")
    gain = norm_gain.reshape(1, D)
    in_hbm = functools.partial(pltpu.with_memory_space_constraint, memory_space=pltpu.HBM)
    gain, query_weight, key_weight, value_weight, out_weight = map(
        in_hbm, (gain, query_weight, key_weight, value_weight, out_weight)
    )

    chips = [(b, z, (x & 2) + a) for b in range(2) for a in range(2)]
    info = [core]
    info += [head_of(b, c, a, core) for b, c, a in chips]
    for b, c, a in chips:
        for half in range(2):
            info.append((((b * 4 + c) * 4 + a) * 2 + (core ^ half)) * ROWS)
    info = jnp.stack(info).astype(jnp.int32)
    info, odd, low, left, ends, front = lax.optimization_barrier(
        (info, near(x) == 1, yl == 0, x < 2, (z & 1) == 0, z < 2)
    )

    other_raw = lax.ppermute(context, "core", SWAP)
    own, query_columns, gain, kv_columns = pl.pallas_call(
        own_kernel,
        out_shape=[shape(ROWS, D), shape(D, 4 * HD), shape(1, D, dtype=F32), shape(D, 8 * HD)],
        in_specs=[SMEM] + [HBM] * 5,
        out_specs=[VMEM] * 4,
        scratch_shapes=[pltpu.VMEM((ROWS, D), BF16), pltpu.SemaphoreType.DMA((14,))],
        compiler_params=params(16),
        cost_estimate=pl.CostEstimate(flops=2**23, bytes_accessed=2**23, transcendentals=0),
    )(info, in_hbm(context), gain, query_weight, key_weight, value_weight)
    other, *queries = pl.pallas_call(
        query_kernel,
        out_shape=[shape(ROWS, D)] + [shape(LAT, HD)] * 4,
        in_specs=[SMEM] + [VMEM] * 4,
        out_specs=[VMEM] * 5,
        compiler_params=params(24),
        cost_estimate=pl.CostEstimate(flops=2**29, bytes_accessed=2**21, transcendentals=0),
    )(info, other_raw, own, gain, query_columns)

    def hop(value, dx, dz, dy):
        pairs = []
        for b in range(2):
            for c in range(4):
                for a in range(4):
                    pairs.append(((b * 4 + c) * 4 + a, ((b ^ dy) * 4 + (c ^ dz)) * 4 + (a ^ dx)))
        return lax.ppermute(value, ("yl", "z", "xh", "xl"), pairs)

    by_x = hop(queries[2], 1, 0, 0)
    by_y = hop(queries[1], 0, 0, 1)
    by_xy = hop(queries[0], 1, 0, 1)

    kv = pl.pallas_call(
        kv_kernel,
        out_shape=shape(4, 2 * ROWS, 2 * HD),
        in_specs=[VMEM] * 3,
        out_specs=HBM,
        scratch_shapes=[pltpu.VMEM((4, 2 * ROWS, 2 * HD), BF16), pltpu.SemaphoreType.DMA((2,))],
        compiler_params=params(24),
        cost_estimate=pl.CostEstimate(flops=2**31, bytes_accessed=2**22, transcendentals=0),
    )(own, other, kv_columns)

    query = jnp.where(
        odd, jnp.where(low, by_xy, by_x), jnp.where(low, by_y, queries[3])
    )
    query, kv = lax.optimization_barrier((query, kv))
    kv = lax.all_to_all(kv, ("yl", "xl"), 0, 0)
    along = [query] + [hop(query, 0, d, 0) for d in (1, 2, 3)]
    out_rows = pl.pallas_call(
        fetch_kernel,
        out_shape=[shape(2 * HD, D)] * FETCHED,
        in_specs=[HBM],
        out_specs=[VMEM] * FETCHED,
        scratch_shapes=[pltpu.SemaphoreType.DMA((FETCHED,))],
        compiler_params=params(16),
        cost_estimate=pl.CostEstimate(flops=1, bytes_accessed=2**26, transcendentals=0),
    )(out_weight)
    query = jnp.where(
        front, jnp.where(ends, along[3], along[2]), jnp.where(ends, along[1], along[0])
    )
    query, *out_rows = lax.optimization_barrier((query, *out_rows))
    across = hop(query, 3, 0, 0)
    query = jnp.where(left, across, query)

    parts = pl.pallas_call(
        attend_kernel,
        out_shape=shape(LAT // 8, 2, 8, HD),
        in_specs=[SMEM] + [VMEM] * 2,
        out_specs=VMEM,
        compiler_params=params(16),
        cost_estimate=pl.CostEstimate(flops=2**28, bytes_accessed=2**21, transcendentals=2**19),
    )(info, query, kv)
    parts = lax.all_to_all(parts.reshape(64, 8, HD), CTX_AXES, 0, 0)
    return pl.pallas_call(
        merge_kernel,
        out_shape=shape(MINE, D),
        in_specs=[VMEM, HBM] + [VMEM] * FETCHED,
        out_specs=VMEM,
        scratch_shapes=[pltpu.VMEM((4 - FETCHED, 2 * HD, D), BF16), pltpu.SemaphoreType.DMA((4,))],
        compiler_params=params(16),
        cost_estimate=pl.CostEstimate(flops=2**25, bytes_accessed=2**22, transcendentals=2**16),
    )(parts, out_weight, *out_rows)


def solution(mesh):
    fine = Mesh(mesh.devices.reshape(2, 4, 2, 2, 2, 2), CTX_AXES + ("batch",))
    rows = P(("batch",) + CTX_AXES, None)
    return jax.shard_map(
        local,
        mesh=fine,
        in_specs=(rows, P(), P(), P(), P(), P()),
        out_specs=rows,
        check_vma=False,
    )
```

```python
import functools

import jax
import jax.numpy as jnp
from jax import lax
from jax.experimental import pallas as pl
from jax.experimental.pallas import tpu as pltpu
from jax.sharding import Mesh
from jax.sharding import PartitionSpec as P

HEADS = 8
HD = 128
D = 2048
LAT = 256
ROWS = 256
CTX = 16384
MINE = 4
FETCHED = 3
F32 = jnp.float32
BF16 = jnp.bfloat16
CTX_AXES = ("yl", "z", "xh", "xl", "core")
SWAP = ((0, 1), (1, 0))
HBM = pl.BlockSpec(memory_space=pltpu.HBM)
VMEM = pl.BlockSpec(memory_space=pltpu.VMEM)
SMEM = pl.BlockSpec(memory_space=pltpu.SMEM)


def near(i):
    return (i ^ (i >> 1)) & 1


def head_of(yl, z, x, core):
    return core * 4 + near(x) * 2 + yl


def params(mib):
    return pltpu.CompilerParams(vmem_limit_bytes=mib * 2**20)


def normalise(tokens, gain):
    widened = tokens.astype(F32)
    centred = widened - jnp.mean(widened, axis=-1, keepdims=True)
    variance = jnp.mean(centred * centred, axis=-1, keepdims=True)
    return (centred * lax.rsqrt(variance + 1e-05) * gain).astype(BF16)


def fetch_heads(weight, heads, dst, offset, sem):
    at = pl.ds(pl.multiple_of(heads * HD, HD), HD)
    copy = pltpu.make_async_copy(weight.at[:, at], dst.at[:, pl.ds(offset, HD)], sem)
    copy.start()
    return copy


def own_kernel(info, tokens, gain_ref, wq, wk, wv, out, columns, gain, kv_columns, rows, sems):
    first = pltpu.make_async_copy(tokens, rows, sems.at[12])
    first.start()
    second = pltpu.make_async_copy(gain_ref, gain, sems.at[13])
    second.start()
    copies = [fetch_heads(wq, info[1 + j], columns, j * HD, sems.at[j]) for j in range(4)]
    for j in range(4):
        for k, weight in enumerate((wk, wv)):
            copies.append(
                fetch_heads(weight, info[1 + j], kv_columns, (2 * j + k) * HD, sems.at[4 + 2 * j + k])
            )
    first.wait()
    second.wait()
    out[...] = normalise(rows[...], gain[...])
    for copy in copies:
        copy.wait()


def query_kernel(info, tokens, own, gain, weight, out, q0, q1, q2, q3):
    out[...] = normalise(tokens[...], gain[...])
    latents = jnp.where(info[0] == 1, own[...], out[...])
    queries = jnp.dot(latents, weight[...], preferred_element_type=F32) * HD ** (-0.5)
    queries = queries.astype(BF16)
    for j, q in enumerate((q0, q1, q2, q3)):
        q[...] = queries[:, j * HD : (j + 1) * HD]


def kv_kernel(own, other, weight, out, done, sems):
    writes = []
    for k, rows in enumerate((own, other)):
        at = pl.ds(k * ROWS, ROWS)
        projected = jnp.dot(rows[...], weight[...], preferred_element_type=F32).astype(BF16)
        for j in range(4):
            done[j, at, :] = projected[:, j * 2 * HD : (j + 1) * 2 * HD]
        writes.append(pltpu.make_async_copy(done.at[:, at], out.at[:, at], sems.at[k]))
        writes[-1].start()
    for write in writes:
        write.wait()


def fetch_rows(wo, pieces, first, sems):
    copies = []
    for j, piece in enumerate(pieces):
        at = pl.ds((first + j) * 2 * HD, 2 * HD)
        copies.append(pltpu.make_async_copy(wo.at[at], piece, sems.at[j]))
        copies[-1].start()
    return copies


def fetch_kernel(wo, *rest):
    *pieces, sems = rest
    for copy in fetch_rows(wo, pieces, 0, sems):
        copy.wait()


def thirds(value):
    first = value.astype(BF16).astype(F32)
    second = (value - first).astype(BF16).astype(F32)
    return [first, second, value - first - second]


def attend_kernel(info, query, kv, wo, out, *rest):
    *pieces, sems = rest
    copies = fetch_rows(wo, pieces, FETCHED, sems)
    queries = query[...]
    row = lax.broadcasted_iota(jnp.int32, (LAT, ROWS), 0)
    column = lax.broadcasted_iota(jnp.int32, (LAT, ROWS), 1)
    lead = column - row
    scores = []
    for j in range(4):
        for half in range(2):
            keys = kv[j, pl.ds(half * ROWS, ROWS), pl.ds(0, HD)]
            part = lax.dot_general(queries, keys, (((1,), (1,)), ((), ())), preferred_element_type=F32)
            room = CTX - LAT - info[5 + 2 * j + half]
            scores.append(jnp.where(lead <= room, part, -jnp.inf))
    peak = functools.reduce(jnp.maximum, scores)
    peak = jnp.max(peak, axis=-1, keepdims=True)
    total = jnp.zeros((LAT, 1), F32)
    accum = jnp.zeros((LAT, HD), F32)
    for j in range(4):
        for half in range(2):
            expo = jnp.exp(scores[2 * j + half] - peak)
            total += jnp.sum(expo, axis=-1, keepdims=True)
            values = kv[j, pl.ds(half * ROWS, ROWS), pl.ds(HD, HD)]
            accum += jnp.dot(expo.astype(BF16), values, preferred_element_type=F32)
    lane = lax.broadcasted_iota(jnp.int32, (LAT, HD), 1)
    stats = jnp.zeros((LAT, HD), F32)
    for k, piece in enumerate(thirds(peak) + thirds(total)):
        stats = jnp.where(lane == k, piece, stats)
    stats = stats.reshape(LAT // 8, 8, HD)
    accum = accum.reshape(LAT // 8, 8, HD)
    upper = lax.broadcasted_iota(jnp.int32, (LAT // 8, 8, HD), 1) < MINE
    out[:, 0] = jnp.where(upper, accum, pltpu.roll(stats, MINE, 1)).astype(BF16)
    out[:, 1] = jnp.where(upper, pltpu.roll(accum, MINE, 1), stats).astype(BF16)
    for copy in copies:
        copy.wait()


def merge_kernel(parts, *rest):
    *pieces, out = rest
    row = lax.broadcasted_iota(jnp.int32, (8, HD), 0) < MINE
    k = lax.broadcasted_iota(jnp.int32, (HD, 2 * HD), 0)
    n = lax.broadcasted_iota(jnp.int32, (HD, 2 * HD), 1)
    lead = k - jnp.where(n < HD, 0, 3)
    pick = jnp.where((lead >= 0) & (lead < 3), 1.0, 0.0).astype(BF16)
    stats = jnp.dot(parts[...].reshape(8 * 64, HD), pick, preferred_element_type=F32)
    stats = stats.reshape(64, 8, 2 * HD)
    members = [[] for _ in range(HEADS)]
    for yl in range(2):
        for z in range(4):
            for x in range(4):
                for core in range(2):
                    members[head_of(yl, z, x, core)].append(((yl * 4 + z) * 4 + x) * 2 + core)
    heads = []
    for group in members:
        accums, peaks, totals = [], [], []
        for source in group:
            block = pltpu.roll(stats[source], MINE, 0)
            accums.append(parts[source].astype(F32))
            peaks.append(block[:, :HD])
            totals.append(block[:, HD:])
        peak = functools.reduce(jnp.maximum, peaks)
        accum = jnp.zeros((8, HD), F32)
        total = jnp.zeros((8, HD), F32)
        for a, p, t in zip(accums, peaks, totals):
            factor = jnp.exp(p - peak)
            accum += a * factor
            total += t * factor
        heads.append(jnp.where(row, accum / total, 0.0).astype(BF16))
    result = jnp.zeros((8, D), F32)
    for j, piece in enumerate(pieces):
        attended = jnp.concatenate(heads[2 * j : 2 * j + 2], axis=1)
        result += jnp.dot(attended, piece[...], preferred_element_type=F32)
    out[...] = result.astype(BF16)[:MINE]


def shape(*dims, dtype=BF16):
    return jax.ShapeDtypeStruct(dims, dtype)


def local(context, norm_gain, query_weight, key_weight, value_weight, out_weight):
    core = lax.axis_index("core")
    x = lax.axis_index(("xh", "xl"))
    z = lax.axis_index("z")
    yl = lax.axis_index("yl")
    gain = norm_gain.reshape(1, D)
    in_hbm = functools.partial(pltpu.with_memory_space_constraint, memory_space=pltpu.HBM)
    gain, query_weight, key_weight, value_weight, out_weight = map(
        in_hbm, (gain, query_weight, key_weight, value_weight, out_weight)
    )

    chips = [(b, z, (x & 2) + a) for b in range(2) for a in range(2)]
    info = [core]
    info += [head_of(b, c, a, core) for b, c, a in chips]
    for b, c, a in chips:
        for half in range(2):
            info.append((((b * 4 + c) * 4 + a) * 2 + (core ^ half)) * ROWS)
    info = jnp.stack(info).astype(jnp.int32)
    info, odd, low, left, ends, front = lax.optimization_barrier(
        (info, near(x) == 1, yl == 0, x < 2, (z & 1) == 0, z < 2)
    )

    other_raw = lax.ppermute(context, "core", SWAP)
    own, query_columns, gain, kv_columns = pl.pallas_call(
        own_kernel,
        out_shape=[shape(ROWS, D), shape(D, 4 * HD), shape(1, D, dtype=F32), shape(D, 8 * HD)],
        in_specs=[SMEM] + [HBM] * 5,
        out_specs=[VMEM] * 4,
        scratch_shapes=[pltpu.VMEM((ROWS, D), BF16), pltpu.SemaphoreType.DMA((14,))],
        compiler_params=params(16),
        cost_estimate=pl.CostEstimate(flops=2**23, bytes_accessed=2**23, transcendentals=0),
    )(info, in_hbm(context), gain, query_weight, key_weight, value_weight)
    other, *queries = pl.pallas_call(
        query_kernel,
        out_shape=[shape(ROWS, D)] + [shape(LAT, HD)] * 4,
        in_specs=[SMEM] + [VMEM] * 4,
        out_specs=[VMEM] * 5,
        compiler_params=params(24),
        cost_estimate=pl.CostEstimate(flops=2**29, bytes_accessed=2**21, transcendentals=0),
    )(info, other_raw, own, gain, query_columns)

    def hop(value, dx, dz, dy):
        pairs = []
        for b in range(2):
            for c in range(4):
                for a in range(4):
                    pairs.append(((b * 4 + c) * 4 + a, ((b ^ dy) * 4 + (c ^ dz)) * 4 + (a ^ dx)))
        return lax.ppermute(value, ("yl", "z", "xh", "xl"), pairs)

    by_x = hop(queries[2], 1, 0, 0)
    by_y = hop(queries[1], 0, 0, 1)
    by_xy = hop(queries[0], 1, 0, 1)

    kv = pl.pallas_call(
        kv_kernel,
        out_shape=shape(4, 2 * ROWS, 2 * HD),
        in_specs=[VMEM] * 3,
        out_specs=HBM,
        scratch_shapes=[pltpu.VMEM((4, 2 * ROWS, 2 * HD), BF16), pltpu.SemaphoreType.DMA((2,))],
        compiler_params=params(24),
        cost_estimate=pl.CostEstimate(flops=2**31, bytes_accessed=2**22, transcendentals=0),
    )(own, other, kv_columns)

    query = jnp.where(
        odd, jnp.where(low, by_xy, by_x), jnp.where(low, by_y, queries[3])
    )
    kv = lax.all_to_all(kv, ("yl", "xl"), 0, 0)
    along = [query] + [hop(query, 0, d, 0) for d in (1, 2, 3)]
    out_rows = pl.pallas_call(
        fetch_kernel,
        out_shape=[shape(2 * HD, D)] * FETCHED,
        in_specs=[HBM],
        out_specs=[VMEM] * FETCHED,
        scratch_shapes=[pltpu.SemaphoreType.DMA((FETCHED,))],
        compiler_params=params(16),
        cost_estimate=pl.CostEstimate(flops=1, bytes_accessed=2**26, transcendentals=0),
    )(out_weight)
    query = jnp.where(
        front, jnp.where(ends, along[3], along[2]), jnp.where(ends, along[1], along[0])
    )
    query, *out_rows = lax.optimization_barrier((query, *out_rows))
    across = hop(query, 3, 0, 0)
    query = jnp.where(left, across, query)

    parts, *more_rows = pl.pallas_call(
        attend_kernel,
        out_shape=[shape(LAT // 8, 2, 8, HD)] + [shape(2 * HD, D)] * (4 - FETCHED),
        in_specs=[SMEM] + [VMEM] * 2 + [HBM],
        out_specs=[VMEM] * (5 - FETCHED),
        scratch_shapes=[pltpu.SemaphoreType.DMA((4 - FETCHED,))],
        compiler_params=params(16),
        cost_estimate=pl.CostEstimate(flops=2**28, bytes_accessed=2**21, transcendentals=2**19),
    )(info, query, kv, out_weight)
    parts = lax.all_to_all(parts.reshape(64, 8, HD), CTX_AXES, 0, 0)
    return pl.pallas_call(
        merge_kernel,
        out_shape=shape(MINE, D),
        in_specs=[VMEM] * 5,
        out_specs=VMEM,
        compiler_params=params(16),
        cost_estimate=pl.CostEstimate(flops=2**25, bytes_accessed=2**22, transcendentals=2**16),
    )(parts, *out_rows, *more_rows)


def solution(mesh):
    fine = Mesh(mesh.devices.reshape(2, 4, 2, 2, 2, 2), CTX_AXES + ("batch",))
    rows = P(("batch",) + CTX_AXES, None)
    return jax.shard_map(
        local,
        mesh=fine,
        in_specs=(rows, P(), P(), P(), P(), P()),
        out_specs=rows,
        check_vma=False,
    )
```

```python
import functools

import jax
import jax.numpy as jnp
from jax import lax
from jax.experimental import pallas as pl
from jax.experimental.pallas import tpu as pltpu
from jax.sharding import Mesh
from jax.sharding import PartitionSpec as P

HEADS = 8
HD = 128
D = 2048
LAT = 256
ROWS = 256
CTX = 16384
MINE = 4
FETCHED = 3
F32 = jnp.float32
BF16 = jnp.bfloat16
CTX_AXES = ("yl", "z", "xh", "xl", "core")
SWAP = ((0, 1), (1, 0))
HBM = pl.BlockSpec(memory_space=pltpu.HBM)
VMEM = pl.BlockSpec(memory_space=pltpu.VMEM)
SMEM = pl.BlockSpec(memory_space=pltpu.SMEM)


def near(i):
    return (i ^ (i >> 1)) & 1


def head_of(yl, z, x, core):
    return core * 4 + near(x) * 2 + yl


def params(mib):
    return pltpu.CompilerParams(vmem_limit_bytes=mib * 2**20)


def mine(info):
    return pl.ds(pl.multiple_of(info[0] * 4 * HD, 4 * HD), 4 * HD)


def normalise(tokens, gain):
    widened = tokens.astype(F32)
    centred = widened - jnp.mean(widened, axis=-1, keepdims=True)
    variance = jnp.mean(centred * centred, axis=-1, keepdims=True)
    return (centred * lax.rsqrt(variance + 1e-05) * gain).astype(BF16)


def own_kernel(info, tokens, gain_ref, wq, out, columns, gain, rows, sems):
    copies = [
        pltpu.make_async_copy(tokens, rows, sems.at[0]),
        pltpu.make_async_copy(gain_ref, gain, sems.at[1]),
        pltpu.make_async_copy(wq.at[:, mine(info)], columns, sems.at[2]),
    ]
    for copy in copies:
        copy.start()
    copies[0].wait()
    copies[1].wait()
    out[...] = normalise(rows[...], gain[...])
    copies[2].wait()


def query_kernel(info, tokens, own, gain, weight, out, q0, q1, q2, q3):
    out[...] = normalise(tokens[...], gain[...])
    latents = jnp.where(info[0] == 1, own[...], out[...])
    queries = jnp.dot(latents, weight[...], preferred_element_type=F32) * HD ** (-0.5)
    queries = queries.astype(BF16)
    for j, q in enumerate((q0, q1, q2, q3)):
        q[...] = queries[:, j * HD : (j + 1) * HD]


def kv_kernel(info, own, other, wk, wv, out, done, sems):
    writes = []
    for k, rows in enumerate((own, other)):
        at = pl.ds(k * ROWS, ROWS)
        keys = jnp.dot(rows[...], wk[:, mine(info)], preferred_element_type=F32).astype(BF16)
        values = jnp.dot(rows[...], wv[:, mine(info)], preferred_element_type=F32).astype(BF16)
        for h in range(4):
            done[h, at, pl.ds(0, HD)] = keys[:, h * HD : (h + 1) * HD]
            done[h, at, pl.ds(HD, HD)] = values[:, h * HD : (h + 1) * HD]
        for h in range(4):
            writes.append(pltpu.make_async_copy(done.at[h, at], out.at[info[1 + h], at], sems.at[4 * k + h]))
            writes[-1].start()
    for write in writes:
        write.wait()


def fetch_rows(wo, pieces, first, sems):
    copies = []
    for j, piece in enumerate(pieces):
        at = pl.ds((first + j) * 2 * HD, 2 * HD)
        copies.append(pltpu.make_async_copy(wo.at[at], piece, sems.at[j]))
        copies[-1].start()
    return copies


def fetch_kernel(wo, *rest):
    *pieces, sems = rest
    for copy in fetch_rows(wo, pieces, 0, sems):
        copy.wait()


def thirds(value):
    first = value.astype(BF16).astype(F32)
    second = (value - first).astype(BF16).astype(F32)
    return [first, second, value - first - second]


def attend_kernel(info, query, kv, wo, out, *rest):
    *pieces, sems = rest
    copies = fetch_rows(wo, pieces, FETCHED, sems)
    queries = query[...]
    row = lax.broadcasted_iota(jnp.int32, (LAT, ROWS), 0)
    column = lax.broadcasted_iota(jnp.int32, (LAT, ROWS), 1)
    lead = column - row
    scores = []
    for j in range(4):
        for half in range(2):
            keys = kv[j, pl.ds(half * ROWS, ROWS), pl.ds(0, HD)]
            part = lax.dot_general(queries, keys, (((1,), (1,)), ((), ())), preferred_element_type=F32)
            room = CTX - LAT - info[5 + 2 * j + half]
            scores.append(jnp.where(lead <= room, part, -jnp.inf))
    peak = functools.reduce(jnp.maximum, scores)
    peak = jnp.max(peak, axis=-1, keepdims=True)
    total = jnp.zeros((LAT, 1), F32)
    accum = jnp.zeros((LAT, HD), F32)
    for j in range(4):
        for half in range(2):
            expo = jnp.exp(scores[2 * j + half] - peak)
            total += jnp.sum(expo, axis=-1, keepdims=True)
            values = kv[j, pl.ds(half * ROWS, ROWS), pl.ds(HD, HD)]
            accum += jnp.dot(expo.astype(BF16), values, preferred_element_type=F32)
    lane = lax.broadcasted_iota(jnp.int32, (LAT, HD), 1)
    stats = jnp.zeros((LAT, HD), F32)
    for k, piece in enumerate(thirds(peak) + thirds(total)):
        stats = jnp.where(lane == k, piece, stats)
    stats = stats.reshape(LAT // 8, 8, HD)
    accum = accum.reshape(LAT // 8, 8, HD)
    upper = lax.broadcasted_iota(jnp.int32, (LAT // 8, 8, HD), 1) < MINE
    out[:, 0] = jnp.where(upper, accum, pltpu.roll(stats, MINE, 1)).astype(BF16)
    out[:, 1] = jnp.where(upper, pltpu.roll(accum, MINE, 1), stats).astype(BF16)
    for copy in copies:
        copy.wait()


def merge_kernel(parts, *rest):
    *pieces, out = rest
    row = lax.broadcasted_iota(jnp.int32, (8, HD), 0) < MINE
    k = lax.broadcasted_iota(jnp.int32, (HD, 2 * HD), 0)
    n = lax.broadcasted_iota(jnp.int32, (HD, 2 * HD), 1)
    lead = k - jnp.where(n < HD, 0, 3)
    pick = jnp.where((lead >= 0) & (lead < 3), 1.0, 0.0).astype(BF16)
    stats = jnp.dot(parts[...].reshape(8 * 64, HD), pick, preferred_element_type=F32)
    stats = stats.reshape(64, 8, 2 * HD)
    members = [[] for _ in range(HEADS)]
    for yl in range(2):
        for z in range(4):
            for x in range(4):
                for core in range(2):
                    members[head_of(yl, z, x, core)].append(((yl * 4 + z) * 4 + x) * 2 + core)
    heads = []
    for group in members:
        accums, peaks, totals = [], [], []
        for source in group:
            block = pltpu.roll(stats[source], MINE, 0)
            accums.append(parts[source].astype(F32))
            peaks.append(block[:, :HD])
            totals.append(block[:, HD:])
        peak = functools.reduce(jnp.maximum, peaks)
        accum = jnp.zeros((8, HD), F32)
        total = jnp.zeros((8, HD), F32)
        for a, p, t in zip(accums, peaks, totals):
            factor = jnp.exp(p - peak)
            accum += a * factor
            total += t * factor
        heads.append(jnp.where(row, accum / total, 0.0).astype(BF16))
    result = jnp.zeros((8, D), F32)
    for j, piece in enumerate(pieces):
        attended = jnp.concatenate(heads[2 * j : 2 * j + 2], axis=1)
        result += jnp.dot(attended, piece[...], preferred_element_type=F32)
    out[...] = result.astype(BF16)[:MINE]


def shape(*dims, dtype=BF16):
    return jax.ShapeDtypeStruct(dims, dtype)


def local(context, norm_gain, query_weight, key_weight, value_weight, out_weight):
    core = lax.axis_index("core")
    x = lax.axis_index(("xh", "xl"))
    z = lax.axis_index("z")
    yl = lax.axis_index("yl")
    gain = norm_gain.reshape(1, D)
    in_hbm = functools.partial(pltpu.with_memory_space_constraint, memory_space=pltpu.HBM)
    gain, query_weight, out_weight = map(in_hbm, (gain, query_weight, out_weight))

    chips = [(b, z, (x & 2) + a) for b in range(2) for a in range(2)]
    info = [core] + [(h & 1) * 2 + ((h >> 1) ^ (x >> 1)) for h in range(4)]
    for b, c, a in chips:
        for half in range(2):
            info.append((((b * 4 + c) * 4 + a) * 2 + (core ^ half)) * ROWS)
    info = jnp.stack(info).astype(jnp.int32)
    info, odd, low, left, ends, front = lax.optimization_barrier(
        (info, near(x) == 1, yl == 0, x < 2, (z & 1) == 0, z < 2)
    )

    other_raw = lax.ppermute(context, "core", SWAP)
    own, query_columns, gain = pl.pallas_call(
        own_kernel,
        out_shape=[shape(ROWS, D), shape(D, 4 * HD), shape(1, D, dtype=F32)],
        in_specs=[SMEM] + [HBM] * 3,
        out_specs=[VMEM] * 3,
        scratch_shapes=[pltpu.VMEM((ROWS, D), BF16), pltpu.SemaphoreType.DMA((3,))],
        compiler_params=params(16),
        cost_estimate=pl.CostEstimate(flops=2**23, bytes_accessed=2**23, transcendentals=0),
    )(info, in_hbm(context), gain, query_weight)
    other, *queries = pl.pallas_call(
        query_kernel,
        out_shape=[shape(ROWS, D)] + [shape(LAT, HD)] * 4,
        in_specs=[SMEM] + [VMEM] * 4,
        out_specs=[VMEM] * 5,
        compiler_params=params(24),
        cost_estimate=pl.CostEstimate(flops=2**29, bytes_accessed=2**21, transcendentals=0),
    )(info, other_raw, own, gain, query_columns)

    def hop(value, dx, dz, dy):
        pairs = []
        for b in range(2):
            for c in range(4):
                for a in range(4):
                    pairs.append(((b * 4 + c) * 4 + a, ((b ^ dy) * 4 + (c ^ dz)) * 4 + (a ^ dx)))
        return lax.ppermute(value, ("yl", "z", "xh", "xl"), pairs)

    by_x = hop(queries[3], 1, 0, 0)
    by_y = hop(queries[0], 0, 0, 1)
    by_xy = hop(queries[2], 1, 0, 1)

    kv = pl.pallas_call(
        kv_kernel,
        out_shape=shape(4, 2 * ROWS, 2 * HD),
        in_specs=[SMEM] + [VMEM] * 4,
        out_specs=HBM,
        scratch_shapes=[pltpu.VMEM((4, 2 * ROWS, 2 * HD), BF16), pltpu.SemaphoreType.DMA((8,))],
        compiler_params=params(24),
        cost_estimate=pl.CostEstimate(flops=2**31, bytes_accessed=2**22, transcendentals=0),
    )(info, own, other, key_weight, value_weight)

    query = jnp.where(
        odd, jnp.where(low, by_xy, by_x), jnp.where(low, by_y, queries[1])
    )
    kv = lax.all_to_all(kv, ("yl", "xl"), 0, 0)
    along = [query] + [hop(query, 0, d, 0) for d in (1, 2, 3)]
    out_rows = pl.pallas_call(
        fetch_kernel,
        out_shape=[shape(2 * HD, D)] * FETCHED,
        in_specs=[HBM],
        out_specs=[VMEM] * FETCHED,
        scratch_shapes=[pltpu.SemaphoreType.DMA((FETCHED,))],
        compiler_params=params(16),
        cost_estimate=pl.CostEstimate(flops=1, bytes_accessed=2**26, transcendentals=0),
    )(out_weight)
    query = jnp.where(
        front, jnp.where(ends, along[3], along[2]), jnp.where(ends, along[1], along[0])
    )
    query, *out_rows = lax.optimization_barrier((query, *out_rows))
    across = hop(query, 3, 0, 0)
    query = jnp.where(left, across, query)

    parts, *more_rows = pl.pallas_call(
        attend_kernel,
        out_shape=[shape(LAT // 8, 2, 8, HD)] + [shape(2 * HD, D)] * (4 - FETCHED),
        in_specs=[SMEM] + [VMEM] * 2 + [HBM],
        out_specs=[VMEM] * (5 - FETCHED),
        scratch_shapes=[pltpu.SemaphoreType.DMA((4 - FETCHED,))],
        compiler_params=params(16),
        cost_estimate=pl.CostEstimate(flops=2**28, bytes_accessed=2**21, transcendentals=2**19),
    )(info, query, kv, out_weight)
    parts = lax.all_to_all(parts.reshape(64, 8, HD), CTX_AXES, 0, 0)
    return pl.pallas_call(
        merge_kernel,
        out_shape=shape(MINE, D),
        in_specs=[VMEM] * 5,
        out_specs=VMEM,
        compiler_params=params(16),
        cost_estimate=pl.CostEstimate(flops=2**25, bytes_accessed=2**22, transcendentals=2**16),
    )(parts, *out_rows, *more_rows)


def solution(mesh):
    fine = Mesh(mesh.devices.reshape(2, 4, 2, 2, 2, 2), CTX_AXES + ("batch",))
    rows = P(("batch",) + CTX_AXES, None)
    return jax.shard_map(
        local,
        mesh=fine,
        in_specs=(rows, P(), P(), P(), P(), P()),
        out_specs=rows,
        check_vma=False,
    )
```

```python
import functools

import jax
import jax.numpy as jnp
from jax import lax
from jax.experimental import pallas as pl
from jax.experimental.pallas import tpu as pltpu
from jax.sharding import Mesh
from jax.sharding import PartitionSpec as P

HEADS = 8
HD = 128
D = 2048
LAT = 256
ROWS = 256
CTX = 16384
MINE = 4
PIECES = 2
FETCHED = 3
F32 = jnp.float32
BF16 = jnp.bfloat16
CTX_AXES = ("yl", "z", "xh", "xl", "core")
SWAP = ((0, 1), (1, 0))
HBM = pl.BlockSpec(memory_space=pltpu.HBM)
VMEM = pl.BlockSpec(memory_space=pltpu.VMEM)
SMEM = pl.BlockSpec(memory_space=pltpu.SMEM)


def near(i):
    return (i ^ (i >> 1)) & 1


def head_of(yl, z, x, core):
    return core * 4 + near(x) * 2 + yl


def params(mib):
    return pltpu.CompilerParams(vmem_limit_bytes=mib * 2**20)


def mine(info):
    return pl.ds(pl.multiple_of(info[0] * 4 * HD, 4 * HD), 4 * HD)


def normalise(tokens, gain):
    widened = tokens.astype(F32)
    centred = widened - jnp.mean(widened, axis=-1, keepdims=True)
    variance = jnp.mean(centred * centred, axis=-1, keepdims=True)
    return (centred * lax.rsqrt(variance + 1e-05) * gain).astype(BF16)


def own_kernel(info, tokens, gain_ref, wk, wv, out, keys, values, gain, rows, sems):
    step = ROWS // PIECES
    pieces = [pl.ds(j * step, step) for j in range(PIECES)]
    first = pltpu.make_async_copy(gain_ref, gain, sems.at[0])
    copies = [pltpu.make_async_copy(tokens.at[at], rows.at[at], sems.at[3 + j]) for j, at in enumerate(pieces)]
    weights = [
        pltpu.make_async_copy(wk.at[:, mine(info)], keys, sems.at[1]),
        pltpu.make_async_copy(wv.at[:, mine(info)], values, sems.at[2]),
    ]
    for copy in (first, *copies, *weights):
        copy.start()
    first.wait()
    for at, copy in zip(pieces, copies):
        copy.wait()
        out[at, :] = normalise(rows[at, :], gain[...])
    for copy in weights:
        copy.wait()


def project_kernel(info, tokens, own, gain, wk, wv, wq, q0, q1, q2, q3, out, other, columns, done, sems):
    fetch = pltpu.make_async_copy(wq.at[:, mine(info)], columns, sems.at[8])
    fetch.start()
    other[...] = normalise(tokens[...], gain[...])
    writes = []
    for k, rows in enumerate((own, other)):
        at = pl.ds(k * ROWS, ROWS)
        keys = jnp.dot(rows[...], wk[...], preferred_element_type=F32).astype(BF16)
        values = jnp.dot(rows[...], wv[...], preferred_element_type=F32).astype(BF16)
        for h in range(4):
            done[h, at, pl.ds(0, HD)] = keys[:, h * HD : (h + 1) * HD]
            done[h, at, pl.ds(HD, HD)] = values[:, h * HD : (h + 1) * HD]
        for h in range(4):
            writes.append(pltpu.make_async_copy(done.at[h, at], out.at[info[1 + h], at], sems.at[4 * k + h]))
            writes[-1].start()
    fetch.wait()
    latents = jnp.where(info[0] == 1, own[...], other[...])
    queries = jnp.dot(latents, columns[...], preferred_element_type=F32) * HD ** (-0.5)
    queries = queries.astype(BF16)
    for j, q in enumerate((q0, q1, q2, q3)):
        q[...] = queries[:, j * HD : (j + 1) * HD]
    for write in writes:
        write.wait()


def fetch_rows(wo, pieces, first, sems):
    copies = []
    for j, piece in enumerate(pieces):
        at = pl.ds((first + j) * 2 * HD, 2 * HD)
        copies.append(pltpu.make_async_copy(wo.at[at], piece, sems.at[j]))
        copies[-1].start()
    return copies


def fetch_kernel(wo, *rest):
    *pieces, sems = rest
    for copy in fetch_rows(wo, pieces, 0, sems):
        copy.wait()


def thirds(value):
    first = value.astype(BF16).astype(F32)
    second = (value - first).astype(BF16).astype(F32)
    return [first, second, value - first - second]


def attend_kernel(info, query, kv, wo, out, *rest):
    *pieces, sems = rest
    copies = fetch_rows(wo, pieces, FETCHED, sems)
    queries = query[...]
    row = lax.broadcasted_iota(jnp.int32, (LAT, ROWS), 0)
    column = lax.broadcasted_iota(jnp.int32, (LAT, ROWS), 1)
    lead = column - row
    scores = []
    for j in range(4):
        for half in range(2):
            keys = kv[j, pl.ds(half * ROWS, ROWS), pl.ds(0, HD)]
            part = lax.dot_general(queries, keys, (((1,), (1,)), ((), ())), preferred_element_type=F32)
            room = CTX - LAT - info[5 + 2 * j + half]
            scores.append(jnp.where(lead <= room, part, -jnp.inf))
    peak = functools.reduce(jnp.maximum, scores)
    peak = jnp.max(peak, axis=-1, keepdims=True)
    total = jnp.zeros((LAT, 1), F32)
    accum = jnp.zeros((LAT, HD), F32)
    for j in range(4):
        for half in range(2):
            expo = jnp.exp(scores[2 * j + half] - peak)
            total += jnp.sum(expo, axis=-1, keepdims=True)
            values = kv[j, pl.ds(half * ROWS, ROWS), pl.ds(HD, HD)]
            accum += jnp.dot(expo.astype(BF16), values, preferred_element_type=F32)
    lane = lax.broadcasted_iota(jnp.int32, (LAT, HD), 1)
    stats = jnp.zeros((LAT, HD), F32)
    for k, piece in enumerate(thirds(peak) + thirds(total)):
        stats = jnp.where(lane == k, piece, stats)
    stats = stats.reshape(LAT // 8, 8, HD)
    accum = accum.reshape(LAT // 8, 8, HD)
    upper = lax.broadcasted_iota(jnp.int32, (LAT // 8, 8, HD), 1) < MINE
    out[:, 0] = jnp.where(upper, accum, pltpu.roll(stats, MINE, 1)).astype(BF16)
    out[:, 1] = jnp.where(upper, pltpu.roll(accum, MINE, 1), stats).astype(BF16)
    for copy in copies:
        copy.wait()


def merge_kernel(parts, *rest):
    *pieces, out = rest
    row = lax.broadcasted_iota(jnp.int32, (8, HD), 0) < MINE
    k = lax.broadcasted_iota(jnp.int32, (HD, 2 * HD), 0)
    n = lax.broadcasted_iota(jnp.int32, (HD, 2 * HD), 1)
    lead = k - jnp.where(n < HD, 0, 3)
    pick = jnp.where((lead >= 0) & (lead < 3), 1.0, 0.0).astype(BF16)
    stats = jnp.dot(parts[...].reshape(8 * 64, HD), pick, preferred_element_type=F32)
    stats = stats.reshape(64, 8, 2 * HD)
    members = [[] for _ in range(HEADS)]
    for yl in range(2):
        for z in range(4):
            for x in range(4):
                for core in range(2):
                    members[head_of(yl, z, x, core)].append(((yl * 4 + z) * 4 + x) * 2 + core)
    heads = []
    for group in members:
        accums, peaks, totals = [], [], []
        for source in group:
            block = pltpu.roll(stats[source], MINE, 0)
            accums.append(parts[source].astype(F32))
            peaks.append(block[:, :HD])
            totals.append(block[:, HD:])
        peak = functools.reduce(jnp.maximum, peaks)
        accum = jnp.zeros((8, HD), F32)
        total = jnp.zeros((8, HD), F32)
        for a, p, t in zip(accums, peaks, totals):
            factor = jnp.exp(p - peak)
            accum += a * factor
            total += t * factor
        heads.append(jnp.where(row, accum / total, 0.0).astype(BF16))
    result = jnp.zeros((8, D), F32)
    for j, piece in enumerate(pieces):
        attended = jnp.concatenate(heads[2 * j : 2 * j + 2], axis=1)
        result += jnp.dot(attended, piece[...], preferred_element_type=F32)
    out[...] = result.astype(BF16)[:MINE]


def shape(*dims, dtype=BF16):
    return jax.ShapeDtypeStruct(dims, dtype)


def local(context, norm_gain, query_weight, key_weight, value_weight, out_weight):
    core = lax.axis_index("core")
    x = lax.axis_index(("xh", "xl"))
    z = lax.axis_index("z")
    yl = lax.axis_index("yl")
    gain = norm_gain.reshape(1, D)
    in_hbm = functools.partial(pltpu.with_memory_space_constraint, memory_space=pltpu.HBM)
    gain, query_weight, key_weight, value_weight, out_weight = map(
        in_hbm, (gain, query_weight, key_weight, value_weight, out_weight)
    )

    chips = [(b, z, (x & 2) + a) for b in range(2) for a in range(2)]
    info = [core] + [(h & 1) * 2 + ((h >> 1) ^ (x >> 1)) for h in range(4)]
    for b, c, a in chips:
        for half in range(2):
            info.append((((b * 4 + c) * 4 + a) * 2 + (core ^ half)) * ROWS)
    info = jnp.stack(info).astype(jnp.int32)
    info, odd, low, left, ends, front = lax.optimization_barrier(
        (info, near(x) == 1, yl == 0, x < 2, (z & 1) == 0, z < 2)
    )

    other_raw = lax.ppermute(context, "core", SWAP)
    own, key_columns, value_columns, gain = pl.pallas_call(
        own_kernel,
        out_shape=[shape(ROWS, D), shape(D, 4 * HD), shape(D, 4 * HD), shape(1, D, dtype=F32)],
        in_specs=[SMEM] + [HBM] * 4,
        out_specs=[VMEM] * 4,
        scratch_shapes=[pltpu.VMEM((ROWS, D), BF16), pltpu.SemaphoreType.DMA((3 + PIECES,))],
        compiler_params=params(16),
        cost_estimate=pl.CostEstimate(flops=2**23, bytes_accessed=2**23, transcendentals=0),
    )(info, in_hbm(context), gain, key_weight, value_weight)
    *queries, kv = pl.pallas_call(
        project_kernel,
        out_shape=[shape(LAT, HD)] * 4 + [shape(4, 2 * ROWS, 2 * HD)],
        in_specs=[SMEM] + [VMEM] * 5 + [HBM],
        out_specs=[VMEM] * 4 + [HBM],
        scratch_shapes=[
            pltpu.VMEM((ROWS, D), BF16),
            pltpu.VMEM((D, 4 * HD), BF16),
            pltpu.VMEM((4, 2 * ROWS, 2 * HD), BF16),
            pltpu.SemaphoreType.DMA((9,)),
        ],
        compiler_params=params(32),
        cost_estimate=pl.CostEstimate(flops=2**31, bytes_accessed=2**22, transcendentals=0),
    )(info, other_raw, own, gain, key_columns, value_columns, query_weight)

    def hop(value, dx, dz, dy):
        pairs = []
        for b in range(2):
            for c in range(4):
                for a in range(4):
                    pairs.append(((b * 4 + c) * 4 + a, ((b ^ dy) * 4 + (c ^ dz)) * 4 + (a ^ dx)))
        return lax.ppermute(value, ("yl", "z", "xh", "xl"), pairs)

    by_x = hop(queries[3], 1, 0, 0)
    by_y = hop(queries[0], 0, 0, 1)
    by_xy = hop(queries[2], 1, 0, 1)

    query = jnp.where(
        odd, jnp.where(low, by_xy, by_x), jnp.where(low, by_y, queries[1])
    )
    kv = lax.all_to_all(kv, ("yl", "xl"), 0, 0)
    along = [query] + [hop(query, 0, d, 0) for d in (1, 2, 3)]
    out_rows = pl.pallas_call(
        fetch_kernel,
        out_shape=[shape(2 * HD, D)] * FETCHED,
        in_specs=[HBM],
        out_specs=[VMEM] * FETCHED,
        scratch_shapes=[pltpu.SemaphoreType.DMA((FETCHED,))],
        compiler_params=params(16),
        cost_estimate=pl.CostEstimate(flops=1, bytes_accessed=2**26, transcendentals=0),
    )(out_weight)
    query = jnp.where(
        front, jnp.where(ends, along[3], along[2]), jnp.where(ends, along[1], along[0])
    )
    query, *out_rows = lax.optimization_barrier((query, *out_rows))
    across = hop(query, 3, 0, 0)
    query = jnp.where(left, across, query)

    parts, *more_rows = pl.pallas_call(
        attend_kernel,
        out_shape=[shape(LAT // 8, 2, 8, HD)] + [shape(2 * HD, D)] * (4 - FETCHED),
        in_specs=[SMEM] + [VMEM] * 2 + [HBM],
        out_specs=[VMEM] * (5 - FETCHED),
        scratch_shapes=[pltpu.SemaphoreType.DMA((4 - FETCHED,))],
        compiler_params=params(16),
        cost_estimate=pl.CostEstimate(flops=2**28, bytes_accessed=2**21, transcendentals=2**19),
    )(info, query, kv, out_weight)
    parts = lax.all_to_all(parts.reshape(64, 8, HD), CTX_AXES, 0, 0)
    return pl.pallas_call(
        merge_kernel,
        out_shape=shape(MINE, D),
        in_specs=[VMEM] * 5,
        out_specs=VMEM,
        compiler_params=params(16),
        cost_estimate=pl.CostEstimate(flops=2**25, bytes_accessed=2**22, transcendentals=2**16),
    )(parts, *out_rows, *more_rows)


def solution(mesh):
    fine = Mesh(mesh.devices.reshape(2, 4, 2, 2, 2, 2), CTX_AXES + ("batch",))
    rows = P(("batch",) + CTX_AXES, None)
    return jax.shard_map(
        local,
        mesh=fine,
        in_specs=(rows, P(), P(), P(), P(), P()),
        out_specs=rows,
        check_vma=False,
    )
```

```python
import functools

import jax
import jax.numpy as jnp
from jax import lax
from jax.experimental import pallas as pl
from jax.experimental.pallas import tpu as pltpu
from jax.sharding import Mesh
from jax.sharding import PartitionSpec as P

HEADS = 8
HD = 128
D = 2048
LAT = 256
ROWS = 256
CTX = 16384
MINE = 4
PIECES = 2
F32 = jnp.float32
BF16 = jnp.bfloat16
CTX_AXES = ("yl", "z", "xh", "xl", "core")
SWAP = ((0, 1), (1, 0))
HBM = pl.BlockSpec(memory_space=pltpu.HBM)
VMEM = pl.BlockSpec(memory_space=pltpu.VMEM)
SMEM = pl.BlockSpec(memory_space=pltpu.SMEM)


def near(i):
    return (i ^ (i >> 1)) & 1


def head_of(yl, z, x, core):
    return core * 4 + near(x) * 2 + yl


def params(mib):
    return pltpu.CompilerParams(vmem_limit_bytes=mib * 2**20)


def mine(info):
    return pl.ds(pl.multiple_of(info[0] * 4 * HD, 4 * HD), 4 * HD)


def normalise(tokens, gain):
    widened = tokens.astype(F32)
    centred = widened - jnp.mean(widened, axis=-1, keepdims=True)
    variance = jnp.mean(centred * centred, axis=-1, keepdims=True)
    return (centred * lax.rsqrt(variance + 1e-05) * gain).astype(BF16)


def own_kernel(info, tokens, gain_ref, wk, wv, out, keys, values, gain, rows, sems):
    step = ROWS // PIECES
    pieces = [pl.ds(j * step, step) for j in range(PIECES)]
    first = pltpu.make_async_copy(gain_ref, gain, sems.at[0])
    copies = [pltpu.make_async_copy(tokens.at[at], rows.at[at], sems.at[3 + j]) for j, at in enumerate(pieces)]
    weights = [
        pltpu.make_async_copy(wk.at[:, mine(info)], keys, sems.at[1]),
        pltpu.make_async_copy(wv.at[:, mine(info)], values, sems.at[2]),
    ]
    for copy in (first, *copies, *weights):
        copy.start()
    first.wait()
    for at, copy in zip(pieces, copies):
        copy.wait()
        out[at, :] = normalise(rows[at, :], gain[...])
    for copy in weights:
        copy.wait()


def project_kernel(info, tokens, own, gain, wk, wv, wq, q0, q1, q2, q3, out, other, columns, done, sems):
    fetch = pltpu.make_async_copy(wq.at[:, mine(info)], columns, sems.at[8])
    fetch.start()
    other[...] = normalise(tokens[...], gain[...])
    writes = []
    for k, rows in enumerate((own, other)):
        at = pl.ds(k * ROWS, ROWS)
        keys = jnp.dot(rows[...], wk[...], preferred_element_type=F32).astype(BF16)
        values = jnp.dot(rows[...], wv[...], preferred_element_type=F32).astype(BF16)
        for h in range(4):
            done[h, at, pl.ds(0, HD)] = keys[:, h * HD : (h + 1) * HD]
            done[h, at, pl.ds(HD, HD)] = values[:, h * HD : (h + 1) * HD]
        for h in range(4):
            writes.append(pltpu.make_async_copy(done.at[h, at], out.at[info[1 + h], at], sems.at[4 * k + h]))
            writes[-1].start()
    fetch.wait()
    latents = jnp.where(info[0] == 1, own[...], other[...])
    queries = jnp.dot(latents, columns[...], preferred_element_type=F32) * HD ** (-0.5)
    queries = queries.astype(BF16)
    for j, q in enumerate((q0, q1, q2, q3)):
        q[...] = queries[:, j * HD : (j + 1) * HD]
    for write in writes:
        write.wait()


def thirds(value):
    first = value.astype(BF16).astype(F32)
    second = (value - first).astype(BF16).astype(F32)
    return [first, second, value - first - second]


def attend_kernel(info, query, kv, out):
    queries = query[...]
    row = lax.broadcasted_iota(jnp.int32, (LAT, ROWS), 0)
    column = lax.broadcasted_iota(jnp.int32, (LAT, ROWS), 1)
    lead = column - row
    scores = []
    for j in range(4):
        for half in range(2):
            keys = kv[j, pl.ds(half * ROWS, ROWS), pl.ds(0, HD)]
            part = lax.dot_general(queries, keys, (((1,), (1,)), ((), ())), preferred_element_type=F32)
            room = CTX - LAT - info[5 + 2 * j + half]
            scores.append(jnp.where(lead <= room, part, -jnp.inf))
    peak = functools.reduce(jnp.maximum, scores)
    peak = jnp.max(peak, axis=-1, keepdims=True)
    total = jnp.zeros((LAT, 1), F32)
    accum = jnp.zeros((LAT, HD), F32)
    for j in range(4):
        for half in range(2):
            expo = jnp.exp(scores[2 * j + half] - peak)
            total += jnp.sum(expo, axis=-1, keepdims=True)
            values = kv[j, pl.ds(half * ROWS, ROWS), pl.ds(HD, HD)]
            accum += jnp.dot(expo.astype(BF16), values, preferred_element_type=F32)
    lane = lax.broadcasted_iota(jnp.int32, (LAT, HD), 1)
    stats = jnp.zeros((LAT, HD), F32)
    for k, piece in enumerate(thirds(peak) + thirds(total)):
        stats = jnp.where(lane == k, piece, stats)
    stats = stats.reshape(LAT // 8, 8, HD)
    accum = accum.reshape(LAT // 8, 8, HD)
    upper = lax.broadcasted_iota(jnp.int32, (LAT // 8, 8, HD), 1) < MINE
    out[:, 0] = jnp.where(upper, accum, pltpu.roll(stats, MINE, 1)).astype(BF16)
    out[:, 1] = jnp.where(upper, pltpu.roll(accum, MINE, 1), stats).astype(BF16)


def merge_kernel(parts, weight, out):
    row = lax.broadcasted_iota(jnp.int32, (8, HD), 0) < MINE
    k = lax.broadcasted_iota(jnp.int32, (HD, 2 * HD), 0)
    n = lax.broadcasted_iota(jnp.int32, (HD, 2 * HD), 1)
    lead = k - jnp.where(n < HD, 0, 3)
    pick = jnp.where((lead >= 0) & (lead < 3), 1.0, 0.0).astype(BF16)
    stats = jnp.dot(parts[...].reshape(8 * 64, HD), pick, preferred_element_type=F32)
    stats = stats.reshape(64, 8, 2 * HD)
    members = [[] for _ in range(HEADS)]
    for yl in range(2):
        for z in range(4):
            for x in range(4):
                for core in range(2):
                    members[head_of(yl, z, x, core)].append(((yl * 4 + z) * 4 + x) * 2 + core)
    heads = []
    for group in members:
        accums, peaks, totals = [], [], []
        for source in group:
            block = pltpu.roll(stats[source], MINE, 0)
            accums.append(parts[source].astype(F32))
            peaks.append(block[:, :HD])
            totals.append(block[:, HD:])
        peak = functools.reduce(jnp.maximum, peaks)
        accum = jnp.zeros((8, HD), F32)
        total = jnp.zeros((8, HD), F32)
        for a, p, t in zip(accums, peaks, totals):
            factor = jnp.exp(p - peak)
            accum += a * factor
            total += t * factor
        heads.append(jnp.where(row, accum / total, 0.0).astype(BF16))
    result = jnp.zeros((8, D), F32)
    for j in range(4):
        attended = jnp.concatenate(heads[2 * j : 2 * j + 2], axis=1)
        rows = weight[pl.ds(j * 2 * HD, 2 * HD), :]
        result += jnp.dot(attended, rows, preferred_element_type=F32)
    out[...] = result.astype(BF16)[:MINE]


def shape(*dims, dtype=BF16):
    return jax.ShapeDtypeStruct(dims, dtype)


def local(context, norm_gain, query_weight, key_weight, value_weight, out_weight):
    core = lax.axis_index("core")
    x = lax.axis_index(("xh", "xl"))
    z = lax.axis_index("z")
    yl = lax.axis_index("yl")
    gain = norm_gain.reshape(1, D)
    in_hbm = functools.partial(pltpu.with_memory_space_constraint, memory_space=pltpu.HBM)
    gain, query_weight, key_weight, value_weight = map(
        in_hbm, (gain, query_weight, key_weight, value_weight)
    )

    chips = [(b, z, (x & 2) + a) for b in range(2) for a in range(2)]
    info = [core] + [(h & 1) * 2 + ((h >> 1) ^ (x >> 1)) for h in range(4)]
    for b, c, a in chips:
        for half in range(2):
            info.append((((b * 4 + c) * 4 + a) * 2 + (core ^ half)) * ROWS)
    info = jnp.stack(info).astype(jnp.int32)
    info, odd, low, left, ends, front = lax.optimization_barrier(
        (info, near(x) == 1, yl == 0, x < 2, (z & 1) == 0, z < 2)
    )

    other_raw = lax.ppermute(context, "core", SWAP)
    own, key_columns, value_columns, gain = pl.pallas_call(
        own_kernel,
        out_shape=[shape(ROWS, D), shape(D, 4 * HD), shape(D, 4 * HD), shape(1, D, dtype=F32)],
        in_specs=[SMEM] + [HBM] * 4,
        out_specs=[VMEM] * 4,
        scratch_shapes=[pltpu.VMEM((ROWS, D), BF16), pltpu.SemaphoreType.DMA((3 + PIECES,))],
        compiler_params=params(16),
        cost_estimate=pl.CostEstimate(flops=2**23, bytes_accessed=2**23, transcendentals=0),
    )(info, in_hbm(context), gain, key_weight, value_weight)
    *queries, kv = pl.pallas_call(
        project_kernel,
        out_shape=[shape(LAT, HD)] * 4 + [shape(4, 2 * ROWS, 2 * HD)],
        in_specs=[SMEM] + [VMEM] * 5 + [HBM],
        out_specs=[VMEM] * 4 + [HBM],
        scratch_shapes=[
            pltpu.VMEM((ROWS, D), BF16),
            pltpu.VMEM((D, 4 * HD), BF16),
            pltpu.VMEM((4, 2 * ROWS, 2 * HD), BF16),
            pltpu.SemaphoreType.DMA((9,)),
        ],
        compiler_params=params(32),
        cost_estimate=pl.CostEstimate(flops=2**31, bytes_accessed=2**22, transcendentals=0),
    )(info, other_raw, own, gain, key_columns, value_columns, query_weight)

    def hop(value, dx, dz, dy):
        pairs = []
        for b in range(2):
            for c in range(4):
                for a in range(4):
                    pairs.append(((b * 4 + c) * 4 + a, ((b ^ dy) * 4 + (c ^ dz)) * 4 + (a ^ dx)))
        return lax.ppermute(value, ("yl", "z", "xh", "xl"), pairs)

    by_x = hop(queries[3], 1, 0, 0)
    by_y = hop(queries[0], 0, 0, 1)
    by_xy = hop(queries[2], 1, 0, 1)

    query = jnp.where(
        odd, jnp.where(low, by_xy, by_x), jnp.where(low, by_y, queries[1])
    )
    kv = lax.all_to_all(kv, ("yl", "xl"), 0, 0)
    along = [query] + [hop(query, 0, d, 0) for d in (1, 2, 3)]
    query = jnp.where(
        front, jnp.where(ends, along[3], along[2]), jnp.where(ends, along[1], along[0])
    )
    across = hop(query, 3, 0, 0)
    query = jnp.where(left, across, query)

    parts = pl.pallas_call(
        attend_kernel,
        out_shape=shape(LAT // 8, 2, 8, HD),
        in_specs=[SMEM] + [VMEM] * 2,
        out_specs=VMEM,
        compiler_params=params(16),
        cost_estimate=pl.CostEstimate(flops=2**33, bytes_accessed=2**21, transcendentals=2**19),
    )(info, query, kv)
    parts = lax.all_to_all(parts.reshape(64, 8, HD), CTX_AXES, 0, 0)
    return pl.pallas_call(
        merge_kernel,
        out_shape=shape(MINE, D),
        in_specs=[VMEM] * 2,
        out_specs=VMEM,
        compiler_params=params(16),
        cost_estimate=pl.CostEstimate(flops=2**25, bytes_accessed=2**22, transcendentals=2**16),
    )(parts, out_weight)


def solution(mesh):
    fine = Mesh(mesh.devices.reshape(2, 4, 2, 2, 2, 2), CTX_AXES + ("batch",))
    rows = P(("batch",) + CTX_AXES, None)
    return jax.shard_map(
        local,
        mesh=fine,
        in_specs=(rows, P(), P(), P(), P(), P()),
        out_specs=rows,
        check_vma=False,
    )
```

```python
import functools

import jax
import jax.numpy as jnp
from jax import lax
from jax.experimental import pallas as pl
from jax.experimental.pallas import tpu as pltpu
from jax.sharding import Mesh
from jax.sharding import PartitionSpec as P

HEADS = 8
HD = 128
D = 2048
LAT = 256
ROWS = 256
CTX = 16384
MINE = 4
PIECES = 2
F32 = jnp.float32
BF16 = jnp.bfloat16
CTX_AXES = ("yl", "z", "xh", "xl", "core")
SWAP = ((0, 1), (1, 0))
HBM = pl.BlockSpec(memory_space=pltpu.HBM)
VMEM = pl.BlockSpec(memory_space=pltpu.VMEM)


def near(i):
    return (i ^ (i >> 1)) & 1


def head_of(yl, z, x, core):
    return core * 4 + near(x) * 2 + yl


def params(mib):
    return pltpu.CompilerParams(vmem_limit_bytes=mib * 2**20)


def places():
    core, z, yl = (lax.axis_index(name) for name in ("core", "z", "yl"))
    xh, xl = lax.axis_index("xh"), lax.axis_index("xl")
    info = [core] + [(h & 1) * 2 + ((h >> 1) ^ xh) for h in range(4)]
    for b in range(2):
        for a in range(2):
            for half in range(2):
                info.append((((b * 4 + z) * 4 + xh * 2 + a) * 2 + (core ^ half)) * ROWS)
    return info


def mine(info):
    return pl.ds(pl.multiple_of(info[0] * 4 * HD, 4 * HD), 4 * HD)


def normalise(tokens, gain):
    widened = tokens.astype(F32)
    centred = widened - jnp.mean(widened, axis=-1, keepdims=True)
    variance = jnp.mean(centred * centred, axis=-1, keepdims=True)
    return (centred * lax.rsqrt(variance + 1e-05) * gain).astype(BF16)


def own_kernel(tokens, gain_ref, wk, wv, out, keys, values, gain, rows, sems):
    info = places()
    step = ROWS // PIECES
    pieces = [pl.ds(j * step, step) for j in range(PIECES)]
    first = pltpu.make_async_copy(gain_ref, gain, sems.at[0])
    copies = [pltpu.make_async_copy(tokens.at[at], rows.at[at], sems.at[3 + j]) for j, at in enumerate(pieces)]
    weights = [
        pltpu.make_async_copy(wk.at[:, mine(info)], keys, sems.at[1]),
        pltpu.make_async_copy(wv.at[:, mine(info)], values, sems.at[2]),
    ]
    for copy in (first, *copies, *weights):
        copy.start()
    first.wait()
    for at, copy in zip(pieces, copies):
        copy.wait()
        out[at, :] = normalise(rows[at, :], gain[...])
    for copy in weights:
        copy.wait()


def project_kernel(tokens, own, gain, wk, wv, wq, q0, q1, q2, q3, out, other, columns, done, sems):
    info = places()
    fetch = pltpu.make_async_copy(wq.at[:, mine(info)], columns, sems.at[8])
    fetch.start()
    other[...] = normalise(tokens[...], gain[...])
    writes = []
    for k, rows in enumerate((own, other)):
        at = pl.ds(k * ROWS, ROWS)
        keys = jnp.dot(rows[...], wk[...], preferred_element_type=F32).astype(BF16)
        values = jnp.dot(rows[...], wv[...], preferred_element_type=F32).astype(BF16)
        for h in range(4):
            done[h, at, pl.ds(0, HD)] = keys[:, h * HD : (h + 1) * HD]
            done[h, at, pl.ds(HD, HD)] = values[:, h * HD : (h + 1) * HD]
        for h in range(4):
            writes.append(pltpu.make_async_copy(done.at[h, at], out.at[info[1 + h], at], sems.at[4 * k + h]))
            writes[-1].start()
    fetch.wait()
    latents = jnp.where(info[0] == 1, own[...], other[...])
    queries = jnp.dot(latents, columns[...], preferred_element_type=F32) * HD ** (-0.5)
    queries = queries.astype(BF16)
    for j, q in enumerate((q0, q1, q2, q3)):
        q[...] = queries[:, j * HD : (j + 1) * HD]
    for write in writes:
        write.wait()


def thirds(value):
    first = value.astype(BF16).astype(F32)
    second = (value - first).astype(BF16).astype(F32)
    return [first, second, value - first - second]


def attend_kernel(query, kv, out):
    info = places()
    queries = query[...]
    row = lax.broadcasted_iota(jnp.int32, (LAT, ROWS), 0)
    column = lax.broadcasted_iota(jnp.int32, (LAT, ROWS), 1)
    lead = column - row
    scores = []
    for j in range(4):
        for half in range(2):
            keys = kv[j, pl.ds(half * ROWS, ROWS), pl.ds(0, HD)]
            part = lax.dot_general(queries, keys, (((1,), (1,)), ((), ())), preferred_element_type=F32)
            room = CTX - LAT - info[5 + 2 * j + half]
            scores.append(jnp.where(lead <= room, part, -jnp.inf))
    peak = functools.reduce(jnp.maximum, scores)
    peak = jnp.max(peak, axis=-1, keepdims=True)
    total = jnp.zeros((LAT, 1), F32)
    accum = jnp.zeros((LAT, HD), F32)
    for j in range(4):
        for half in range(2):
            expo = jnp.exp(scores[2 * j + half] - peak)
            total += jnp.sum(expo, axis=-1, keepdims=True)
            values = kv[j, pl.ds(half * ROWS, ROWS), pl.ds(HD, HD)]
            accum += jnp.dot(expo.astype(BF16), values, preferred_element_type=F32)
    lane = lax.broadcasted_iota(jnp.int32, (LAT, HD), 1)
    stats = jnp.zeros((LAT, HD), F32)
    for k, piece in enumerate(thirds(peak) + thirds(total)):
        stats = jnp.where(lane == k, piece, stats)
    stats = stats.reshape(LAT // 8, 8, HD)
    accum = accum.reshape(LAT // 8, 8, HD)
    upper = lax.broadcasted_iota(jnp.int32, (LAT // 8, 8, HD), 1) < MINE
    out[:, 0] = jnp.where(upper, accum, pltpu.roll(stats, MINE, 1)).astype(BF16)
    out[:, 1] = jnp.where(upper, pltpu.roll(accum, MINE, 1), stats).astype(BF16)


def merge_kernel(parts, weight, out):
    row = lax.broadcasted_iota(jnp.int32, (8, HD), 0) < MINE
    k = lax.broadcasted_iota(jnp.int32, (HD, 2 * HD), 0)
    n = lax.broadcasted_iota(jnp.int32, (HD, 2 * HD), 1)
    lead = k - jnp.where(n < HD, 0, 3)
    pick = jnp.where((lead >= 0) & (lead < 3), 1.0, 0.0).astype(BF16)
    stats = jnp.dot(parts[...].reshape(8 * 64, HD), pick, preferred_element_type=F32)
    stats = stats.reshape(64, 8, 2 * HD)
    members = [[] for _ in range(HEADS)]
    for yl in range(2):
        for z in range(4):
            for x in range(4):
                for core in range(2):
                    members[head_of(yl, z, x, core)].append(((yl * 4 + z) * 4 + x) * 2 + core)
    heads = []
    for group in members:
        accums, peaks, totals = [], [], []
        for source in group:
            block = pltpu.roll(stats[source], MINE, 0)
            accums.append(parts[source].astype(F32))
            peaks.append(block[:, :HD])
            totals.append(block[:, HD:])
        peak = functools.reduce(jnp.maximum, peaks)
        accum = jnp.zeros((8, HD), F32)
        total = jnp.zeros((8, HD), F32)
        for a, p, t in zip(accums, peaks, totals):
            factor = jnp.exp(p - peak)
            accum += a * factor
            total += t * factor
        heads.append(jnp.where(row, accum / total, 0.0).astype(BF16))
    result = jnp.zeros((8, D), F32)
    for j in range(4):
        attended = jnp.concatenate(heads[2 * j : 2 * j + 2], axis=1)
        rows = weight[pl.ds(j * 2 * HD, 2 * HD), :]
        result += jnp.dot(attended, rows, preferred_element_type=F32)
    out[...] = result.astype(BF16)[:MINE]


def shape(*dims, dtype=BF16):
    return jax.ShapeDtypeStruct(dims, dtype)


def local(context, norm_gain, query_weight, key_weight, value_weight, out_weight):
    x = lax.axis_index(("xh", "xl"))
    z = lax.axis_index("z")
    yl = lax.axis_index("yl")
    gain = norm_gain.reshape(1, D)
    in_hbm = functools.partial(pltpu.with_memory_space_constraint, memory_space=pltpu.HBM)
    gain, query_weight, key_weight, value_weight = map(
        in_hbm, (gain, query_weight, key_weight, value_weight)
    )

    gain, odd, left, ends, front, low = lax.optimization_barrier(
        (gain, near(x) == 1, x < 2, (z & 1) == 0, z < 2, yl == 0)
    )

    other_raw = lax.ppermute(context, "core", SWAP)
    own, key_columns, value_columns, gain = pl.pallas_call(
        own_kernel,
        out_shape=[shape(ROWS, D), shape(D, 4 * HD), shape(D, 4 * HD), shape(1, D, dtype=F32)],
        in_specs=[HBM] * 4,
        out_specs=[VMEM] * 4,
        scratch_shapes=[pltpu.VMEM((ROWS, D), BF16), pltpu.SemaphoreType.DMA((3 + PIECES,))],
        compiler_params=params(16),
        cost_estimate=pl.CostEstimate(flops=2**23, bytes_accessed=2**23, transcendentals=0),
    )(in_hbm(context), gain, key_weight, value_weight)
    *queries, kv = pl.pallas_call(
        project_kernel,
        out_shape=[shape(LAT, HD)] * 4 + [shape(4, 2 * ROWS, 2 * HD)],
        in_specs=[VMEM] * 5 + [HBM],
        out_specs=[VMEM] * 4 + [HBM],
        scratch_shapes=[
            pltpu.VMEM((ROWS, D), BF16),
            pltpu.VMEM((D, 4 * HD), BF16),
            pltpu.VMEM((4, 2 * ROWS, 2 * HD), BF16),
            pltpu.SemaphoreType.DMA((9,)),
        ],
        compiler_params=params(32),
        cost_estimate=pl.CostEstimate(flops=2**31, bytes_accessed=2**22, transcendentals=0),
    )(other_raw, own, gain, key_columns, value_columns, query_weight)

    def hop(value, dx, dz, dy):
        pairs = []
        for b in range(2):
            for c in range(4):
                for a in range(4):
                    pairs.append(((b * 4 + c) * 4 + a, ((b ^ dy) * 4 + (c ^ dz)) * 4 + (a ^ dx)))
        return lax.ppermute(value, ("yl", "z", "xh", "xl"), pairs)

    by_x = hop(queries[3], 1, 0, 0)
    by_y = hop(queries[0], 0, 0, 1)
    by_xy = hop(queries[2], 1, 0, 1)

    query = jnp.where(
        odd, jnp.where(low, by_xy, by_x), jnp.where(low, by_y, queries[1])
    )
    kv = lax.all_to_all(kv, ("yl", "xl"), 0, 0)
    along = [query] + [hop(query, 0, d, 0) for d in (1, 2, 3)]
    query = jnp.where(
        front, jnp.where(ends, along[3], along[2]), jnp.where(ends, along[1], along[0])
    )
    across = hop(query, 3, 0, 0)
    query = jnp.where(left, across, query)

    parts = pl.pallas_call(
        attend_kernel,
        out_shape=shape(LAT // 8, 2, 8, HD),
        in_specs=[VMEM] * 2,
        out_specs=VMEM,
        compiler_params=params(16),
        cost_estimate=pl.CostEstimate(flops=2**33, bytes_accessed=2**21, transcendentals=2**19),
    )(query, kv)
    parts = lax.all_to_all(parts.reshape(64, 8, HD), CTX_AXES, 0, 0)
    return pl.pallas_call(
        merge_kernel,
        out_shape=shape(MINE, D),
        in_specs=[VMEM] * 2,
        out_specs=VMEM,
        compiler_params=params(16),
        cost_estimate=pl.CostEstimate(flops=2**25, bytes_accessed=2**22, transcendentals=2**16),
    )(parts, out_weight)


def solution(mesh):
    fine = Mesh(mesh.devices.reshape(2, 4, 2, 2, 2, 2), CTX_AXES + ("batch",))
    rows = P(("batch",) + CTX_AXES, None)
    return jax.shard_map(
        local,
        mesh=fine,
        in_specs=(rows, P(), P(), P(), P(), P()),
        out_specs=rows,
        check_vma=False,
    )
```

```python
import functools

import jax
import jax.numpy as jnp
from jax import lax
from jax.experimental import pallas as pl
from jax.experimental.pallas import tpu as pltpu
from jax.sharding import Mesh
from jax.sharding import PartitionSpec as P

HEADS = 8
HD = 128
D = 2048
LAT = 256
ROWS = 256
CTX = 16384
MINE = 4
PIECES = 2
F32 = jnp.float32
BF16 = jnp.bfloat16
CTX_AXES = ("yl", "z", "xh", "xl", "core")
SWAP = ((0, 1), (1, 0))
HBM = pl.BlockSpec(memory_space=pltpu.HBM)
VMEM = pl.BlockSpec(memory_space=pltpu.VMEM)


def near(i):
    return (i ^ (i >> 1)) & 1


def head_of(yl, z, x, core):
    return core * 4 + near(x) * 2 + yl


def params(mib):
    return pltpu.CompilerParams(vmem_limit_bytes=mib * 2**20)


def places():
    core, z, yl = (lax.axis_index(name) for name in ("core", "z", "yl"))
    xh, xl = lax.axis_index("xh"), lax.axis_index("xl")
    info = [core] + [(h & 1) * 2 + ((h >> 1) ^ xh) for h in range(4)]
    for b in range(2):
        for a in range(2):
            for half in range(2):
                info.append((((b * 4 + z) * 4 + xh * 2 + a) * 2 + (core ^ half)) * ROWS)
    return info


def mine(info):
    return pl.ds(pl.multiple_of(info[0] * 4 * HD, 4 * HD), 4 * HD)


def normalise(tokens, gain):
    widened = tokens.astype(F32)
    centred = widened - jnp.mean(widened, axis=-1, keepdims=True)
    variance = jnp.mean(centred * centred, axis=-1, keepdims=True)
    return (centred * lax.rsqrt(variance + 1e-05) * gain).astype(BF16)


def own_kernel(tokens, gain_ref, wk, wv, out, keys, values, gain, rows, sems):
    info = places()
    step = ROWS // PIECES
    pieces = [pl.ds(j * step, step) for j in range(PIECES)]
    first = pltpu.make_async_copy(gain_ref, gain, sems.at[0])
    copies = [pltpu.make_async_copy(tokens.at[at], rows.at[at], sems.at[3 + j]) for j, at in enumerate(pieces)]
    weights = [
        pltpu.make_async_copy(wk.at[:, mine(info)], keys, sems.at[1]),
        pltpu.make_async_copy(wv.at[:, mine(info)], values, sems.at[2]),
    ]
    for copy in (first, *copies, *weights):
        copy.start()
    first.wait()
    for at, copy in zip(pieces, copies):
        copy.wait()
        out[at, :] = normalise(rows[at, :], gain[...])
    for copy in weights:
        copy.wait()


def project_kernel(tokens, own, gain, wk, wv, wq, q0, q1, q2, q3, out, other, columns, done, sems):
    info = places()
    fetch = pltpu.make_async_copy(wq.at[:, mine(info)], columns, sems.at[8])
    fetch.start()
    writes = []
    for k, rows in enumerate((own, other)):
        if k == 1:
            other[...] = normalise(tokens[...], gain[...])
        at = pl.ds(k * ROWS, ROWS)
        keys = jnp.dot(rows[...], wk[...], preferred_element_type=F32).astype(BF16)
        values = jnp.dot(rows[...], wv[...], preferred_element_type=F32).astype(BF16)
        for h in range(4):
            done[h, at, pl.ds(0, HD)] = keys[:, h * HD : (h + 1) * HD]
            done[h, at, pl.ds(HD, HD)] = values[:, h * HD : (h + 1) * HD]
        for h in range(4):
            writes.append(pltpu.make_async_copy(done.at[h, at], out.at[info[1 + h], at], sems.at[4 * k + h]))
            writes[-1].start()
    fetch.wait()
    latents = jnp.where(info[0] == 1, own[...], other[...])
    queries = jnp.dot(latents, columns[...], preferred_element_type=F32) * HD ** (-0.5)
    queries = queries.astype(BF16)
    for j, q in enumerate((q0, q1, q2, q3)):
        q[...] = queries[:, j * HD : (j + 1) * HD]
    for write in writes:
        write.wait()


def thirds(value):
    first = value.astype(BF16).astype(F32)
    second = (value - first).astype(BF16).astype(F32)
    return [first, second, value - first - second]


def attend_kernel(query, kv, out):
    info = places()
    queries = query[...]
    row = lax.broadcasted_iota(jnp.int32, (LAT, ROWS), 0)
    column = lax.broadcasted_iota(jnp.int32, (LAT, ROWS), 1)
    lead = column - row
    scores = []
    for j in range(4):
        for half in range(2):
            keys = kv[j, pl.ds(half * ROWS, ROWS), pl.ds(0, HD)]
            part = lax.dot_general(queries, keys, (((1,), (1,)), ((), ())), preferred_element_type=F32)
            room = CTX - LAT - info[5 + 2 * j + half]
            scores.append(jnp.where(lead <= room, part, -jnp.inf))
    peak = functools.reduce(jnp.maximum, scores)
    peak = jnp.max(peak, axis=-1, keepdims=True)
    total = jnp.zeros((LAT, 1), F32)
    accum = jnp.zeros((LAT, HD), F32)
    for j in range(4):
        for half in range(2):
            expo = jnp.exp(scores[2 * j + half] - peak)
            total += jnp.sum(expo, axis=-1, keepdims=True)
            values = kv[j, pl.ds(half * ROWS, ROWS), pl.ds(HD, HD)]
            accum += jnp.dot(expo.astype(BF16), values, preferred_element_type=F32)
    lane = lax.broadcasted_iota(jnp.int32, (LAT, HD), 1)
    stats = jnp.zeros((LAT, HD), F32)
    for k, piece in enumerate(thirds(peak) + thirds(total)):
        stats = jnp.where(lane == k, piece, stats)
    stats = stats.reshape(LAT // 8, 8, HD)
    accum = accum.reshape(LAT // 8, 8, HD)
    upper = lax.broadcasted_iota(jnp.int32, (LAT // 8, 8, HD), 1) < MINE
    out[:, 0] = jnp.where(upper, accum, pltpu.roll(stats, MINE, 1)).astype(BF16)
    out[:, 1] = jnp.where(upper, pltpu.roll(accum, MINE, 1), stats).astype(BF16)


def merge_kernel(parts, weight, out):
    row = lax.broadcasted_iota(jnp.int32, (8, HD), 0) < MINE
    k = lax.broadcasted_iota(jnp.int32, (HD, 2 * HD), 0)
    n = lax.broadcasted_iota(jnp.int32, (HD, 2 * HD), 1)
    lead = k - jnp.where(n < HD, 0, 3)
    pick = jnp.where((lead >= 0) & (lead < 3), 1.0, 0.0).astype(BF16)
    stats = jnp.dot(parts[...].reshape(8 * 64, HD), pick, preferred_element_type=F32)
    stats = stats.reshape(64, 8, 2 * HD)
    members = [[] for _ in range(HEADS)]
    for yl in range(2):
        for z in range(4):
            for x in range(4):
                for core in range(2):
                    members[head_of(yl, z, x, core)].append(((yl * 4 + z) * 4 + x) * 2 + core)
    heads = []
    for group in members:
        accums, peaks, totals = [], [], []
        for source in group:
            block = pltpu.roll(stats[source], MINE, 0)
            accums.append(parts[source].astype(F32))
            peaks.append(block[:, :HD])
            totals.append(block[:, HD:])
        peak = functools.reduce(jnp.maximum, peaks)
        accum = jnp.zeros((8, HD), F32)
        total = jnp.zeros((8, HD), F32)
        for a, p, t in zip(accums, peaks, totals):
            factor = jnp.exp(p - peak)
            accum += a * factor
            total += t * factor
        heads.append(jnp.where(row, accum / total, 0.0).astype(BF16))
    result = jnp.zeros((8, D), F32)
    for j in range(4):
        attended = jnp.concatenate(heads[2 * j : 2 * j + 2], axis=1)
        rows = weight[pl.ds(j * 2 * HD, 2 * HD), :]
        result += jnp.dot(attended, rows, preferred_element_type=F32)
    out[...] = result.astype(BF16)[:MINE]


def shape(*dims, dtype=BF16):
    return jax.ShapeDtypeStruct(dims, dtype)


def local(context, norm_gain, query_weight, key_weight, value_weight, out_weight):
    x = lax.axis_index(("xh", "xl"))
    z = lax.axis_index("z")
    yl = lax.axis_index("yl")
    gain = norm_gain.reshape(1, D)
    in_hbm = functools.partial(pltpu.with_memory_space_constraint, memory_space=pltpu.HBM)
    gain, query_weight, key_weight, value_weight = map(
        in_hbm, (gain, query_weight, key_weight, value_weight)
    )

    gain, odd, left, ends, front, low = lax.optimization_barrier(
        (gain, near(x) == 1, x < 2, (z & 1) == 0, z < 2, yl == 0)
    )

    other_raw = lax.ppermute(context, "core", SWAP)
    own, key_columns, value_columns, gain = pl.pallas_call(
        own_kernel,
        out_shape=[shape(ROWS, D), shape(D, 4 * HD), shape(D, 4 * HD), shape(1, D, dtype=F32)],
        in_specs=[HBM] * 4,
        out_specs=[VMEM] * 4,
        scratch_shapes=[pltpu.VMEM((ROWS, D), BF16), pltpu.SemaphoreType.DMA((3 + PIECES,))],
        compiler_params=params(16),
        cost_estimate=pl.CostEstimate(flops=2**23, bytes_accessed=2**23, transcendentals=0),
    )(in_hbm(context), gain, key_weight, value_weight)
    *queries, kv = pl.pallas_call(
        project_kernel,
        out_shape=[shape(LAT, HD)] * 4 + [shape(4, 2 * ROWS, 2 * HD)],
        in_specs=[VMEM] * 5 + [HBM],
        out_specs=[VMEM] * 4 + [HBM],
        scratch_shapes=[
            pltpu.VMEM((ROWS, D), BF16),
            pltpu.VMEM((D, 4 * HD), BF16),
            pltpu.VMEM((4, 2 * ROWS, 2 * HD), BF16),
            pltpu.SemaphoreType.DMA((9,)),
        ],
        compiler_params=params(32),
        cost_estimate=pl.CostEstimate(flops=2**31, bytes_accessed=2**22, transcendentals=0),
    )(other_raw, own, gain, key_columns, value_columns, query_weight)

    def hop(value, dx, dz, dy):
        pairs = []
        for b in range(2):
            for c in range(4):
                for a in range(4):
                    pairs.append(((b * 4 + c) * 4 + a, ((b ^ dy) * 4 + (c ^ dz)) * 4 + (a ^ dx)))
        return lax.ppermute(value, ("yl", "z", "xh", "xl"), pairs)

    by_x = hop(queries[3], 1, 0, 0)
    by_y = hop(queries[0], 0, 0, 1)
    by_xy = hop(queries[2], 1, 0, 1)

    query = jnp.where(
        odd, jnp.where(low, by_xy, by_x), jnp.where(low, by_y, queries[1])
    )
    kv = lax.all_to_all(kv, ("yl", "xl"), 0, 0)
    along = [query] + [hop(query, 0, d, 0) for d in (1, 2, 3)]
    query = jnp.where(
        front, jnp.where(ends, along[3], along[2]), jnp.where(ends, along[1], along[0])
    )
    across = hop(query, 3, 0, 0)
    query = jnp.where(left, across, query)

    parts = pl.pallas_call(
        attend_kernel,
        out_shape=shape(LAT // 8, 2, 8, HD),
        in_specs=[VMEM] * 2,
        out_specs=VMEM,
        compiler_params=params(16),
        cost_estimate=pl.CostEstimate(flops=2**33, bytes_accessed=2**21, transcendentals=2**19),
    )(query, kv)
    parts = lax.all_to_all(parts.reshape(64, 8, HD), CTX_AXES, 0, 0)
    return pl.pallas_call(
        merge_kernel,
        out_shape=shape(MINE, D),
        in_specs=[VMEM] * 2,
        out_specs=VMEM,
        compiler_params=params(16),
        cost_estimate=pl.CostEstimate(flops=2**25, bytes_accessed=2**22, transcendentals=2**16),
    )(parts, out_weight)


def solution(mesh):
    fine = Mesh(mesh.devices.reshape(2, 4, 2, 2, 2, 2), CTX_AXES + ("batch",))
    rows = P(("batch",) + CTX_AXES, None)
    return jax.shard_map(
        local,
        mesh=fine,
        in_specs=(rows, P(), P(), P(), P(), P()),
        out_specs=rows,
        check_vma=False,
    )
```
